512 devices in a mesh: spec: 8 (over y_hi, core), frow: 8 (over y_lo, x), fcol: 8 (over z).
Axes of the slice: x: 4, y: 8 (y_hi: 4, y_lo: 2; y = y_hi * 2 + y_lo), z: 8, core: 2. Of those that a mesh axis runs over, the one named last changes fastest.
Arguments:
- primal_slab: float32 [96, 16, 8, 8, 1024], P('spec', None, 'frow', 'fcol'), may hold values from -8 to 8
- wave_dual: float32 [96, 1024, 1024], P('spec', 'frow', 'fcol'), may hold values from -3 to 3
- nuc_dual: float32 [96, 1024, 1024], P('spec', 'frow', 'fcol'), may hold values from -3 to 3
- l21_weights: float32 [2, 1024, 1024], P(None, 'frow', 'fcol'), may hold values from 2.078461 to 20.784609
- nuc_thresh: float32 [8, 8, 8], P('frow', 'fcol'), may hold values from 32 to 320
- basis: float32 [8, 8, 96, 8], P('frow', 'fcol', 'spec'), may hold values from -0.625 to 0.625
- band_of: int32 [8, 8, 96], P('frow', 'fcol', 'spec'), may hold values from 0 to 1
- margin_width: int32 [8, 8, 2], P('frow', 'fcol'), may hold values from 10 to 21
Outputs:
- wave_new: float32 [96, 1024, 1024], P('spec', 'frow', 'fcol')
- nuc_new: float32 [96, 1024, 1024], P('spec', 'frow', 'fcol')
The draws below stay inside these ranges and needn't reach their ends.
All inputs are finite; a program needn't handle non-finite values.
Results may differ from the reference program's by a relative error of at most 0.0003.
Values sent between devices are 32-bit elements; how exact they have to be, the bound alone decides.
No kernel may reach another device: no remote copies, remote signals or barrier semaphores. Data moves between devices by JAX's collectives and lax.ppermute only.
A program may use at most 128 MiB of HBM per device.

```python
import math
import jax
import jax.numpy as jnp
from jax import lax

BANDS = 2
RANK = 8
HALO = 21
FH = 128
FW = 128
CHANS = 96
NX = 1024
NY = 1024
FACET_ROWS = 8
FACET_COLS = 8
DEALT = 16


def draw_primal_slab(key, part):
    key = jax.random.fold_in(key, 11)
    first_key = jax.random.fold_in(key, 0)
    full_shape = (CHANS, DEALT, FACET_ROWS, FACET_COLS, NY)
    channel = jnp.arange(CHANS, dtype=jnp.float32) / float(max(CHANS - 1, 1))
    spectrum = jnp.exp(-math.log(3.0) * channel).reshape(CHANS, 1, 1, 1, 1)
    values = jnp.clip(jax.random.normal(first_key, full_shape, jnp.float32), -6.0, 6.0) * spectrum
    return values


def with_ends(entries, stream_key, low, largest):
    longest = entries.shape.index(max(entries.shape))
    spots = []
    for shift in (0, 1):
        where = [jax.random.randint(jax.random.fold_in(stream_key, axis), (), 0, length) for axis, length in enumerate(entries.shape)]
        where[longest] = (where[longest] + shift) % entries.shape[longest]
        spots.append(tuple(where))
    return entries.at[spots[0]].set(low).at[spots[1]].set(largest)


def levels(own_key, extent, shards, low, largest):
    def one(axis_at, shards_of):
        draws = jax.random.uniform(jax.random.fold_in(jax.random.fold_in(own_key, 6), axis_at), (shards_of,), jnp.float32, low / len(shards), largest / len(shards))
        return jnp.repeat(jnp.exp(draws), extent[axis_at] // shards_of).reshape((-1,) + (1,) * (len(extent) - axis_at - 1))

    loudness = one(*shards[0])
    for cut in shards[1:]:
        loudness = loudness * one(*cut)
    return loudness


def noise(own_key, shape, width, limit, cuts=(), kind=jnp.bfloat16):
    loudness = levels(own_key, shape, cuts, -0.22, 0.18) if cuts else 1.0
    drawn = jax.random.normal(own_key, shape, jnp.float32) * width * loudness
    return jnp.minimum(jnp.maximum(drawn, -limit), limit).astype(kind)


def setup_inputs(seed: int = 0) -> dict:
    splits = jax.random.split(jax.random.key(seed), 9)
    return {
        "primal_slab": draw_primal_slab(jax.random.fold_in(splits[8], 71), 0),
        "wave_dual": noise(splits[1], (CHANS, NX, NY), 0.5, 3.0, ((0, 8), (1, 8), (2, 8)), jnp.float32),
        "nuc_dual": noise(splits[2], (CHANS, NX, NY), 0.5, 3.0, ((0, 8), (1, 8), (2, 8)), jnp.float32),
        "l21_weights": jnp.clip(jnp.exp(math.log(20.784609) - 2.3025851 * jax.random.uniform(splits[3], (BANDS, NX, NY), jnp.float32) ** levels(splits[3], (BANDS, NX, NY), ((1, 8), (2, 8)), -0.2, 0.2)), 2.078461, 20.784609),
        "nuc_thresh": jnp.clip(jnp.exp(math.log(320.0) - 2.3025851 * jax.random.uniform(splits[4], (FACET_ROWS, FACET_COLS, RANK), jnp.float32) ** levels(splits[4], (FACET_ROWS, FACET_COLS, RANK), ((0, 8), (1, 8)), -0.2, 0.2)), 32.0, 320.0),
        "basis": noise(splits[5], (FACET_ROWS, FACET_COLS, CHANS, RANK), CHANS ** -0.5, 0.625, ((0, 8), (1, 8), (2, 8)), jnp.float32),
        "band_of": with_ends(jax.random.randint(splits[6], (FACET_ROWS, FACET_COLS, CHANS), 0, BANDS), jax.random.fold_in(splits[6], 1), 0, BANDS - 1).astype(jnp.int32),
        "margin_width": with_ends(jax.random.randint(splits[7], (FACET_ROWS, FACET_COLS, 2), HALO // 2, HALO + 1), jax.random.fold_in(splits[7], 1), HALO // 2, HALO).astype(jnp.int32),
    }


low_taps = [-0.00011747678400228192, 0.0006754494059985568, -0.0003917403729959771, -0.00487035299301066, 0.008746094047015655, 0.013981027917015516, -0.04408825393106472, -0.01736930100202211, 0.128747426620186, 0.00047248457399797254, -0.2840155429624281, -0.015829105256023893, 0.5853546836548691, 0.6756307362980128, 0.3128715909144659, 0.05441584224308161]
tap_lag = 7
highest = lax.Precision.HIGHEST

def high_taps():
    return [(-1.0) ** place * low_taps[15 - place] for place in range(16)]

def filter_axis(signal, filter_taps, out_first, out_count, along):
    summed = None
    for place in range(16):
        begin_at = 2 * out_first + place
        strided = lax.slice_in_dim(signal, begin_at, begin_at + 2 * (out_count - 1) + 1, 2, along)
        partial_term = filter_taps[place] * strided
        summed = partial_term if summed is None else summed + partial_term
    return summed

def analyse(extended, facet_rows, facet_cols):
    high = high_taps()
    vert_low = filter_axis(extended, low_taps, 0, facet_rows // 2 + 14, 1)
    vert_high = filter_axis(extended, high, tap_lag, facet_rows // 2, 1)
    level_ll = filter_axis(vert_low, low_taps, 0, facet_cols // 2 + 14, 2)
    level_lh = filter_axis(vert_low[:, tap_lag:tap_lag + facet_rows // 2], high, tap_lag, facet_cols // 2, 2)
    level_hl = filter_axis(vert_high, low_taps, tap_lag, facet_cols // 2, 2)
    level_hh = filter_axis(vert_high, high, tap_lag, facet_cols // 2, 2)
    second_low = filter_axis(level_ll, low_taps, 0, facet_rows // 4, 1)
    second_high = filter_axis(level_ll, high, 0, facet_rows // 4, 1)
    coarse_ll = filter_axis(second_low, low_taps, 0, facet_cols // 4, 2)
    coarse_lh = filter_axis(second_low, high, 0, facet_cols // 4, 2)
    coarse_hl = filter_axis(second_high, low_taps, 0, facet_cols // 4, 2)
    coarse_hh = filter_axis(second_high, high, 0, facet_cols // 4, 2)
    coarse = jnp.concatenate([jnp.concatenate([coarse_ll, coarse_lh], axis=2), jnp.concatenate([coarse_hl, coarse_hh], axis=2)], axis=1)
    upper_half = jnp.concatenate([coarse, level_lh], axis=2)
    lower_half = jnp.concatenate([level_hl, level_hh], axis=2)
    return jnp.concatenate([upper_half, lower_half], axis=1)

def window_mask(widths, facet_rows, facet_cols):
    row_pos = jnp.arange(facet_rows + 2 * HALO, dtype=jnp.int32)
    col_pos = jnp.arange(facet_cols + 2 * HALO, dtype=jnp.int32)
    row_in = (row_pos >= HALO - widths[0]) & (row_pos < HALO + facet_rows + widths[0])
    col_in = (col_pos >= HALO - widths[1]) & (col_pos < HALO + facet_cols + widths[1])
    return row_in[:, None] & col_in[None, :]

def shrink_spectrum(combined, spectrum, local_basis, thresholds):
    singular = jnp.sqrt(lax.optimization_barrier(jnp.sum(spectrum * spectrum, axis=(1, 2))))
    retained = thresholds / jnp.maximum(singular, thresholds)
    scaled = spectrum * (1.0 - retained)[:, None, None]
    return combined - jnp.einsum('cr,rij->cij', local_basis, scaled, precision=highest)

def reference(primal_slab, wave_dual, nuc_dual, l21_weights, nuc_thresh, basis, band_of, margin_width):
    channels = primal_slab.shape[0]
    full_image = primal_slab.reshape(channels, NX, NY)
    padded = jnp.pad(full_image, ((0, 0), (HALO, HALO), (HALO, HALO)))
    zero_at = jnp.zeros((), jnp.int32)

    def facet_step(row_index, col_index):
        top_at = (row_index * FH).astype(jnp.int32)
        left_at = (col_index * FW).astype(jnp.int32)
        extended = lax.dynamic_slice(padded, (zero_at, top_at, left_at), (channels, FH + 2 * HALO, FW + 2 * HALO))
        inside = window_mask(margin_width[row_index, col_index], FH, FW)
        extended = jnp.where(inside[None], extended, 0.0)
        dual_sum = lax.dynamic_slice(wave_dual, (zero_at, top_at, left_at), (channels, FH, FW)) + analyse(extended, FH, FW)
        onehot = (band_of[row_index, col_index][None, :] == jnp.arange(BANDS, dtype=jnp.int32)[:, None]).astype(jnp.float32)
        band_sq = jnp.einsum('bc,cij->bij', onehot, dual_sum * dual_sum, precision=highest)
        weights_here = lax.dynamic_slice(l21_weights, (zero_at, top_at, left_at), (BANDS, FH, FW))
        shrink_ratio = weights_here / jnp.maximum(jnp.sqrt(band_sq), weights_here)
        wave_new = dual_sum * jnp.einsum('bc,bij->cij', onehot, shrink_ratio, precision=highest)
        facet_block = lax.dynamic_slice(full_image, (zero_at, top_at, left_at), (channels, FH, FW))
        combined = lax.dynamic_slice(nuc_dual, (zero_at, top_at, left_at), (channels, FH, FW)) + facet_block
        local_basis = basis[row_index, col_index]
        spectrum = jnp.einsum('cr,cij->rij', local_basis, combined, precision=highest)
        nuc_new = shrink_spectrum(combined, spectrum, local_basis, nuc_thresh[row_index, col_index])
        return (wave_new, nuc_new)

    def facet_row(row_index):

        def facet_col(col_index):
            return facet_step(row_index, col_index)
        return lax.map(facet_col, jnp.arange(FACET_COLS, dtype=jnp.int32))
    wave_parts, nuc_parts = lax.map(facet_row, jnp.arange(FACET_ROWS, dtype=jnp.int32))
    wave_new = wave_parts.transpose(2, 0, 3, 1, 4).reshape(channels, NX, NY)
    nuc_new = nuc_parts.transpose(2, 0, 3, 1, 4).reshape(channels, NX, NY)
    return (wave_new, nuc_new)
```

```python
import functools

import jax
import jax.numpy as jnp
import numpy as np
from jax import lax
from jax.experimental import pallas as pl
from jax.experimental.pallas import tpu as pltpu
from jax.sharding import PartitionSpec as P

HALO = 21
EDGE = 24
SLOTS = 3
LANES = 128
FACET = 128
EXT = FACET + 2 * EDGE
VMEM = pl.BlockSpec(memory_space=pltpu.VMEM)
SMEM = pl.BlockSpec(memory_space=pltpu.SMEM)

low_taps = [
    -0.00011747678400228192,
    0.0006754494059985568,
    -0.0003917403729959771,
    -0.00487035299301066,
    0.008746094047015655,
    0.013981027917015516,
    -0.04408825393106472,
    -0.01736930100202211,
    0.128747426620186,
    0.00047248457399797254,
    -0.2840155429624281,
    -0.015829105256023893,
    0.5853546836548691,
    0.6756307362980128,
    0.3128715909144659,
    0.05441584224308161,
]
tap_lag = 7
high_taps = [(-1.0) ** place * low_taps[15 - place] for place in range(16)]


def filter_matrix(in_length, taps, first, count):
    matrix = np.zeros((count, in_length))
    for out in range(count):
        matrix[out, 2 * (out + first) : 2 * (out + first) + 16] = taps
    return matrix


@functools.cache
def operators():
    length = FACET + 2 * HALO
    half, quarter = FACET // 2, FACET // 4
    low_all = filter_matrix(length, low_taps, 0, half + 14)
    high = filter_matrix(length, high_taps, tap_lag, half)
    low = low_all[tap_lag : tap_lag + half]
    coarse = np.concatenate(
        [
            filter_matrix(half + 14, low_taps, 0, quarter) @ low_all,
            filter_matrix(half + 14, high_taps, 0, quarter) @ low_all,
        ]
    )
    return coarse, low, high


def row_operator():
    whole = np.concatenate(operators())
    placed = np.zeros((whole.shape[0], 2 * LANES), np.float32)
    placed[:, :FACET] = whole[:, HALO : HALO + FACET]
    placed[:, FACET + EDGE - HALO : FACET + EDGE] = whole[:, :HALO]
    placed[:, FACET + EDGE : FACET + EDGE + HALO] = whole[:, HALO + FACET :]
    return placed


def column_operators():
    coarse, low, high = operators()
    whole = np.concatenate([coarse, high, low, high]).T.astype(np.float32)
    sides = np.zeros((2, EDGE, 2 * LANES), np.float32)
    sides[0, :HALO] = whole[:HALO]
    sides[1, :HALO] = whole[HALO + FACET :]
    return whole[HALO : HALO + FACET], sides


def split(values):
    head = values.astype(jnp.bfloat16)
    return head, (values - head.astype(jnp.float32)).astype(jnp.bfloat16)


def pack_kernel(rows_ref, out_ref, *, chans, facet_rows, facet_cols, deal):
    block = deal * (chans + chans // SLOTS)
    per_chan = deal * facet_rows * facet_cols
    for i in range(facet_rows):
        for q in range(deal):
            for j in range(facet_cols):
                first = (deal * i + q) * facet_cols + j
                out_ref[pl.ds((i * facet_cols + j) * block + q * chans, chans), :] = rows_ref[
                    pl.ds(first, chans, stride=per_chan), :
                ]
    lane = lax.broadcasted_iota(jnp.int32, (per_chan, LANES), 1)
    column = lax.broadcasted_iota(jnp.int32, (per_chan, LANES), 0) % facet_cols
    for group in range(chans // SLOTS):
        left = jnp.zeros((per_chan, LANES), jnp.float32)
        right = jnp.zeros((per_chan, LANES), jnp.float32)
        on_left = lane < 0
        for slot in range(SLOTS):
            rows = rows_ref[pl.ds((group * SLOTS + slot) * per_chan, per_chan), :]
            start = 2 * HALO * slot
            here = (lane >= start) & (lane < start + HALO)
            on_left = on_left | here
            left = jnp.where(here, pltpu.roll(rows, (start + HALO) % LANES, 1), left)
            here = (lane >= start + HALO) & (lane < start + 2 * HALO)
            right = jnp.where(here, pltpu.roll(rows, start + HALO, 1), right)
        left = jnp.where(column > 0, pltpu.roll(left, 1, 0), 0.0)
        right = jnp.where(column < facet_cols - 1, pltpu.roll(right, per_chan - 1, 0), 0.0)
        sides = jnp.where(on_left, left, right)
        for i in range(facet_rows):
            for q in range(deal):
                first = (deal * i + q) * facet_cols
                place = i * facet_cols * block + deal * chans + q * (chans // SLOTS) + group
                out_ref[pl.ds(place, facet_cols, stride=block), :] = sides[first : first + facet_cols]


def prepare_kernel(width_ref, rows_ref, centre_ref, sides_ref, v_ref, w_ref, pad):
    lane = lax.broadcasted_iota(jnp.int32, rows_ref.shape, 1)
    up = (lane < FACET) | ((lane >= FACET + EDGE - width_ref[0]) & (lane < FACET + EDGE + width_ref[0]))
    head, tail = split(jnp.where(up, rows_ref[...], 0.0))
    v_ref[:, : 2 * LANES] = head
    v_ref[:, 2 * LANES : 4 * LANES] = tail
    v_ref[:, 4 * LANES :] = head
    place = lax.broadcasted_iota(jnp.int32, sides_ref.shape[1:], 0)
    before = jnp.where(place >= HALO - width_ref[1], sides_ref[0], 0.0)[:HALO]
    after = jnp.where(place < width_ref[1], sides_ref[1], 0.0)[:HALO]
    centre_head, centre_tail = split(centre_ref[...])
    for slot in range(SLOTS):
        pad[...] = jnp.zeros_like(pad)
        pad[2 * HALO * slot : 2 * HALO * slot + HALO, :] = before
        pad[2 * HALO * slot + HALO : 2 * HALO * (slot + 1), :] = after
        head, tail = split(pad[...])
        w_ref[slot] = jnp.concatenate(
            [centre_head, head, centre_head, head, centre_tail, tail], axis=0
        )


def unpack_kernel(in_ref, facet_ref, side_ref, top_ref, bottom_ref, *, chans, deal, senders):
    groups = chans // SLOTS
    block = deal * (chans + groups)
    for at in range(chans + groups):
        if at < chans:
            starts = [q * chans + at for q in range(deal)]
        else:
            starts = [deal * chans + q * groups + at - chans for q in range(deal)]
        rows = jnp.concatenate([in_ref[pl.ds(s, senders, stride=block), :] for s in starts], axis=0)
        if at < chans:
            facet_ref[at] = rows
        else:
            side_ref[at - chans] = rows
        top_ref[at] = rows[:EDGE]
        bottom_ref[at] = rows[FACET - EDGE :]


def project_kernel(facet_ref, nuc_ref, basis_ref, combined_ref, out_ref, *, chans, rank):
    for part in range(0, FACET, 32):
        rows = pl.ds(part, 32)
        total = [None] * rank
        for ch in range(chans):
            block = nuc_ref[ch, rows, :] + facet_ref[ch, rows, :]
            combined_ref[ch, rows, :] = block
            for k in range(rank):
                term = basis_ref[ch, k] * block
                total[k] = term if total[k] is None else total[k] + term
        for k in range(rank):
            out_ref[k, rows, :] = total[k]


def wavelet_kernel(
    band_ref, facet_ref, side_ref, above_ref, below_ref, v_ref, w_ref, wave_ref, out_ref, sq_ref, *, chans
):
    groups = chans // SLOTS
    half = FACET // 2
    lane = lax.broadcasted_iota(jnp.int32, (half, LANES), 1)
    nothing = jnp.zeros((2 * LANES - EXT, 2 * LANES), jnp.bfloat16)
    sides = [
        split(jnp.concatenate([side_ref[g], above_ref[chans + g], below_ref[chans + g]], axis=0))
        for g in range(groups)
    ]
    sq_ref[...] = jnp.zeros_like(sq_ref)
    for slot in range(SLOTS):
        for group in range(groups):
            ch = group * SLOTS + slot
            rows = jnp.concatenate([facet_ref[ch], above_ref[ch], below_ref[ch]], axis=0)
            head, tail = split(rows)
            side_head, side_tail = sides[group]
            taken = jnp.concatenate([head, side_head, tail, side_tail, head, side_head], axis=1)
            across = jnp.dot(taken, w_ref[slot], preferred_element_type=jnp.float32)
            head, tail = split(across)
            stacked = jnp.concatenate([head, nothing, head, nothing, tail, nothing], axis=0)
            both = jnp.dot(v_ref[...], stacked, preferred_element_type=jnp.float32)
            upper = jnp.where(lane < half, both[:half, :LANES], both[half:FACET, :LANES])
            coeffs = jnp.concatenate([upper, both[FACET:, LANES:]], axis=0)
            dual = wave_ref[ch] + coeffs
            out_ref[ch] = dual
            band = band_ref[ch]
            sq_ref[band] = sq_ref[band] + dual * dual


def gate_kernel(first_ref, held_ref, out_ref):
    pass


def weigh_kernel(me_ref, thresh_ref, weight_ref, parts_ref, squares_ref, out_ref, *, per, copies):
    for k in range(per):
        total = parts_ref[0, k]
        for source in range(1, copies):
            total = total + parts_ref[source, k]
        threshold = thresh_ref[me_ref[0] * per + k]
        singular = jnp.sqrt(jnp.sum(total * total, keepdims=True))
        scaled = total * (1.0 - threshold / jnp.maximum(singular, threshold))
        for target in range(copies):
            out_ref[target, k * FACET : (k + 1) * FACET] = scaled
    total = squares_ref[0]
    for source in range(1, copies):
        total = total + squares_ref[source]
    weight = weight_ref[me_ref[0]]
    ratio = weight / jnp.maximum(jnp.sqrt(total), weight)
    for target in range(copies):
        out_ref[target, per * FACET :] = ratio


def finish_kernel(
    band_ref, basis_ref, combined_ref, dual_ref, all_ref, wave_ref, nuc_ref, *, chans, rank, bands, per
):
    share = all_ref.shape[1] - per * FACET
    pieces = FACET // share if share <= FACET else 1
    size = min(share, 32)
    for part in range(0, FACET, size):
        rows = pl.ds(part, size)
        scaled = [all_ref[k // per, pl.ds(k % per * FACET + part, size), :] for k in range(rank)]
        for ch in range(chans):
            total = basis_ref[ch, 0] * scaled[0]
            for k in range(1, rank):
                total = total + basis_ref[ch, k] * scaled[k]
            nuc_ref[ch, rows, :] = combined_ref[ch, rows, :] - total
            source = band_ref[ch] * pieces + part // share
            ratio = all_ref[source, pl.ds(per * FACET + part % share, size), :]
            wave_ref[ch, rows, :] = dual_ref[ch, rows, :] * ratio


def call(kernel, name, ins, outs, operands, scratch=(), flops=0, limit=24):
    size = sum(4 * int(np.prod(o.shape)) for o in outs) + sum(4 * int(np.prod(o.shape)) for o in operands)
    return pl.pallas_call(
        kernel,
        name=name,
        in_specs=ins,
        out_specs=[VMEM] * len(outs),
        out_shape=outs,
        scratch_shapes=list(scratch),
        compiler_params=pltpu.CompilerParams(vmem_limit_bytes=limit * 1024 * 1024),
        cost_estimate=pl.CostEstimate(flops=flops, bytes_accessed=size, transcendentals=0),
    )(*operands)


def f32(*shape):
    return jax.ShapeDtypeStruct(shape, jnp.float32)


def bf16(*shape):
    return jax.ShapeDtypeStruct(shape, jnp.bfloat16)


def shards(primal_slab, wave_dual, nuc_dual, l21_weights, nuc_thresh, basis, band_of, margin_width):
    chans = wave_dual.shape[0]
    spec, rows, cols = (lax.axis_size(a) for a in ("spec", "frow", "fcol"))
    senders = rows * cols
    deal = primal_slab.shape[1] // rows
    rank = basis.shape[3]
    bands = l21_weights.shape[0]
    plane = ("frow", "fcol")
    me = lax.axis_index("spec").astype(jnp.int32).reshape(1)
    local_basis = basis.reshape(chans, rank)
    bands_here = band_of.reshape(chans)
    widths = margin_width.reshape(2)

    groups = chans // SLOTS
    block = deal * (chans + groups)
    (packed,) = call(
        functools.partial(pack_kernel, chans=chans, facet_rows=rows, facet_cols=cols, deal=deal),
        "pack", [VMEM], [f32(senders * block, LANES)],
        [primal_slab.reshape(-1, LANES)],
    )
    arrived = lax.all_to_all(
        packed.reshape(senders, block, LANES), plane, split_axis=0, concat_axis=0, tiled=True
    )
    centre, sides = column_operators()
    vertical, across = call(
        prepare_kernel, "prepare", [SMEM, VMEM, VMEM, VMEM],
        [bf16(3 * FACET // 2, 6 * LANES), bf16(SLOTS, 6 * LANES, 2 * LANES)],
        [widths, jnp.asarray(row_operator()), jnp.asarray(centre), jnp.asarray(sides)],
        scratch=[pltpu.VMEM((LANES, 2 * LANES), jnp.float32)],
    )
    strip = f32(chans + groups, EDGE, LANES)
    facet, side, top, bottom = call(
        functools.partial(unpack_kernel, chans=chans, deal=deal, senders=senders),
        "unpack", [VMEM],
        [f32(chans, FACET, LANES), f32(groups, FACET, LANES), strip, strip],
        [arrived.reshape(-1, LANES)],
    )
    above = lax.ppermute(bottom, "frow", [(i, i + 1) for i in range(rows - 1)])
    below = lax.ppermute(top, "frow", [(i + 1, i) for i in range(rows - 1)])
    combined, partial = call(
        functools.partial(project_kernel, chans=chans, rank=rank),
        "project", [VMEM, VMEM, SMEM],
        [f32(chans, FACET, LANES), f32(rank, FACET, LANES)],
        [facet, nuc_dual, local_basis],
        flops=2 * chans * rank * FACET * LANES,
    )
    per = rank // spec
    share = bands * FACET // spec
    parts = lax.all_to_all(
        partial.reshape(spec, per * FACET, LANES), "spec", split_axis=0, concat_axis=0, tiled=True
    )
    dual_sum, band_part = call(
        functools.partial(wavelet_kernel, chans=chans),
        "wavelet", [SMEM] + [VMEM] * 7,
        [f32(chans, FACET, LANES), f32(bands, FACET, LANES)],
        [bands_here, facet, side, above, below, vertical, across, wave_dual],
        flops=2 * chans * 3 * 192 * 256 * 600,
    )
    band_part = pl.pallas_call(
        gate_kernel,
        name="gate",
        in_specs=[pl.BlockSpec(memory_space=pl.ANY)] * 2,
        out_specs=pl.BlockSpec(memory_space=pl.ANY),
        out_shape=f32(bands, FACET, LANES),
        input_output_aliases={1: 0},
    )(parts, band_part)
    squares = lax.all_to_all(
        band_part.reshape(spec, share, LANES), "spec", split_axis=0, concat_axis=0, tiled=True
    )
    (weighed,) = call(
        functools.partial(weigh_kernel, per=per, copies=spec),
        "weigh", [SMEM, SMEM, VMEM, VMEM, VMEM], [f32(spec, per * FACET + share, LANES)],
        [me, nuc_thresh.reshape(rank), l21_weights.reshape(spec, share, LANES),
         parts.reshape(spec, per, FACET, LANES), squares],
    )
    everyone = lax.all_to_all(weighed, "spec", split_axis=0, concat_axis=0, tiled=True)
    wave_new, nuc_new = call(
        functools.partial(finish_kernel, chans=chans, rank=rank, bands=bands, per=per),
        "finish", [SMEM, SMEM, VMEM, VMEM, VMEM],
        [f32(chans, FACET, LANES), f32(chans, FACET, LANES)],
        [bands_here, local_basis, combined, dual_sum, everyone],
        flops=2 * chans * rank * FACET * LANES,
    )
    return (wave_new, nuc_new)


def solution(mesh):
    return jax.shard_map(
        shards,
        mesh=mesh,
        in_specs=(
            P("spec", None, "frow", "fcol", None),
            P("spec", "frow", "fcol"),
            P("spec", "frow", "fcol"),
            P(None, "frow", "fcol"),
            P("frow", "fcol", None),
            P("frow", "fcol", "spec", None),
            P("frow", "fcol", "spec"),
            P("frow", "fcol", None),
        ),
        out_specs=(P("spec", "frow", "fcol"), P("spec", "frow", "fcol")),
        check_vma=False,
    )
```

```python
import functools

import jax
import jax.numpy as jnp
import numpy as np
from jax import lax
from jax.experimental import pallas as pl
from jax.experimental.pallas import tpu as pltpu
from jax.sharding import PartitionSpec as P

HALO = 21
EDGE = 24
SLOTS = 3
LANES = 128
FACET = 128
EXT = FACET + 2 * EDGE
VMEM = pl.BlockSpec(memory_space=pltpu.VMEM)
SMEM = pl.BlockSpec(memory_space=pltpu.SMEM)
ANY = pl.BlockSpec(memory_space=pl.ANY)

low_taps = [
    -0.00011747678400228192,
    0.0006754494059985568,
    -0.0003917403729959771,
    -0.00487035299301066,
    0.008746094047015655,
    0.013981027917015516,
    -0.04408825393106472,
    -0.01736930100202211,
    0.128747426620186,
    0.00047248457399797254,
    -0.2840155429624281,
    -0.015829105256023893,
    0.5853546836548691,
    0.6756307362980128,
    0.3128715909144659,
    0.05441584224308161,
]
tap_lag = 7
high_taps = [(-1.0) ** place * low_taps[15 - place] for place in range(16)]


def filter_matrix(in_length, taps, first, count):
    matrix = np.zeros((count, in_length))
    for out in range(count):
        matrix[out, 2 * (out + first) : 2 * (out + first) + 16] = taps
    return matrix


@functools.cache
def operators():
    length = FACET + 2 * HALO
    half, quarter = FACET // 2, FACET // 4
    low_all = filter_matrix(length, low_taps, 0, half + 14)
    high = filter_matrix(length, high_taps, tap_lag, half)
    low = low_all[tap_lag : tap_lag + half]
    coarse = np.concatenate(
        [
            filter_matrix(half + 14, low_taps, 0, quarter) @ low_all,
            filter_matrix(half + 14, high_taps, 0, quarter) @ low_all,
        ]
    )
    return coarse, low, high


def row_operator():
    whole = np.concatenate(operators())
    placed = np.zeros((whole.shape[0], 2 * LANES), np.float32)
    placed[:, :FACET] = whole[:, HALO : HALO + FACET]
    placed[:, FACET + EDGE - HALO : FACET + EDGE] = whole[:, :HALO]
    placed[:, FACET + EDGE : FACET + EDGE + HALO] = whole[:, HALO + FACET :]
    return placed


def column_operators():
    coarse, low, high = operators()
    whole = np.concatenate([coarse, high, low, high]).T.astype(np.float32)
    sides = np.zeros((2, EDGE, 2 * LANES), np.float32)
    sides[0, :HALO] = whole[:HALO]
    sides[1, :HALO] = whole[HALO + FACET :]
    return whole[HALO : HALO + FACET], sides


def split(values):
    head = values.astype(jnp.bfloat16)
    return head, (values - head.astype(jnp.float32)).astype(jnp.bfloat16)


def pack_kernel(rows_ref, out_ref, *, chans, facet_rows, facet_cols, deal):
    block = deal * (chans + chans // SLOTS)
    per_chan = deal * facet_rows * facet_cols
    for i in range(facet_rows):
        for q in range(deal):
            for j in range(facet_cols):
                first = (deal * i + q) * facet_cols + j
                out_ref[pl.ds((i * facet_cols + j) * block + q * chans, chans), :] = rows_ref[
                    pl.ds(first, chans, stride=per_chan), :
                ]
    lane = lax.broadcasted_iota(jnp.int32, (per_chan, LANES), 1)
    column = lax.broadcasted_iota(jnp.int32, (per_chan, LANES), 0) % facet_cols
    for group in range(chans // SLOTS):
        left = jnp.zeros((per_chan, LANES), jnp.float32)
        right = jnp.zeros((per_chan, LANES), jnp.float32)
        on_left = lane < 0
        for slot in range(SLOTS):
            rows = rows_ref[pl.ds((group * SLOTS + slot) * per_chan, per_chan), :]
            start = 2 * HALO * slot
            here = (lane >= start) & (lane < start + HALO)
            on_left = on_left | here
            left = jnp.where(here, pltpu.roll(rows, (start + HALO) % LANES, 1), left)
            here = (lane >= start + HALO) & (lane < start + 2 * HALO)
            right = jnp.where(here, pltpu.roll(rows, start + HALO, 1), right)
        left = jnp.where(column > 0, pltpu.roll(left, 1, 0), 0.0)
        right = jnp.where(column < facet_cols - 1, pltpu.roll(right, per_chan - 1, 0), 0.0)
        sides = jnp.where(on_left, left, right)
        for i in range(facet_rows):
            for q in range(deal):
                first = (deal * i + q) * facet_cols
                place = i * facet_cols * block + deal * chans + q * (chans // SLOTS) + group
                out_ref[pl.ds(place, facet_cols, stride=block), :] = sides[first : first + facet_cols]


def prepare_kernel(width_ref, rows_ref, centre_ref, sides_ref, v_ref, w_ref, pad):
    lane = lax.broadcasted_iota(jnp.int32, rows_ref.shape, 1)
    up = (lane < FACET) | ((lane >= FACET + EDGE - width_ref[0]) & (lane < FACET + EDGE + width_ref[0]))
    head, tail = split(jnp.where(up, rows_ref[...], 0.0))
    v_ref[:, : 2 * LANES] = head
    v_ref[:, 2 * LANES : 4 * LANES] = tail
    v_ref[:, 4 * LANES :] = head
    place = lax.broadcasted_iota(jnp.int32, sides_ref.shape[1:], 0)
    before = jnp.where(place >= HALO - width_ref[1], sides_ref[0], 0.0)[:HALO]
    after = jnp.where(place < width_ref[1], sides_ref[1], 0.0)[:HALO]
    centre_head, centre_tail = split(centre_ref[...])
    for slot in range(SLOTS):
        pad[...] = jnp.zeros_like(pad)
        pad[2 * HALO * slot : 2 * HALO * slot + HALO, :] = before
        pad[2 * HALO * slot + HALO : 2 * HALO * (slot + 1), :] = after
        head, tail = split(pad[...])
        w_ref[slot] = jnp.concatenate(
            [centre_head, head, centre_head, head, centre_tail, tail], axis=0
        )


def unpack_kernel(in_ref, facet_ref, side_ref, top_ref, bottom_ref, *, chans, deal, senders):
    groups = chans // SLOTS
    block = deal * (chans + groups)
    for at in range(chans + groups):
        if at < chans:
            starts = [q * chans + at for q in range(deal)]
        else:
            starts = [deal * chans + q * groups + at - chans for q in range(deal)]
        rows = jnp.concatenate([in_ref[pl.ds(s, senders, stride=block), :] for s in starts], axis=0)
        if at < chans:
            facet_ref[at] = rows
        else:
            side_ref[at - chans] = rows
        top_ref[at] = rows[:EDGE]
        bottom_ref[at] = rows[FACET - EDGE :]


def project_kernel(facet_ref, nuc_ref, basis_ref, combined_ref, out_ref, *, chans, rank):
    for part in range(0, FACET, 32):
        rows = pl.ds(part, 32)
        total = [None] * rank
        for ch in range(chans):
            block = nuc_ref[ch, rows, :] + facet_ref[ch, rows, :]
            combined_ref[ch, rows, :] = block
            for k in range(rank):
                term = basis_ref[k, ch] * block
                total[k] = term if total[k] is None else total[k] + term
        for k in range(rank):
            out_ref[k, rows, :] = total[k]


def wavelet_kernel(
    band_ref, facet_ref, side_ref, above_ref, below_ref, v_ref, w_ref, partial_ref, wave_ref,
    out_ref, sums_ref, wave, squares, sems, *, chans,
):
    fetches = [pltpu.make_async_copy(wave_ref.at[ch], wave.at[ch], sems.at[ch]) for ch in range(chans)]
    for fetch in fetches:
        fetch.start()
    copies, height = sums_ref.shape[0], sums_ref.shape[1]
    taken_rows = partial_ref.shape[1]
    sums_ref[:, :taken_rows, :] = partial_ref[...]
    squares[...] = jnp.zeros_like(squares)
    groups = chans // SLOTS
    half = FACET // 2
    lane = lax.broadcasted_iota(jnp.int32, (half, LANES), 1)
    nothing = jnp.zeros((2 * LANES - EXT, 2 * LANES), jnp.bfloat16)
    sides = [
        split(jnp.concatenate([side_ref[g], above_ref[chans + g], below_ref[chans + g]], axis=0))
        for g in range(groups)
    ]
    for slot in range(SLOTS):
        for group in range(groups):
            ch = group * SLOTS + slot
            rows = jnp.concatenate([facet_ref[ch], above_ref[ch], below_ref[ch]], axis=0)
            head, tail = split(rows)
            side_head, side_tail = sides[group]
            taken = jnp.concatenate([head, side_head, tail, side_tail, head, side_head], axis=1)
            across = jnp.dot(taken, w_ref[slot], preferred_element_type=jnp.float32)
            head, tail = split(across)
            stacked = jnp.concatenate([head, nothing, head, nothing, tail, nothing], axis=0)
            both = jnp.dot(v_ref[...], stacked, preferred_element_type=jnp.float32)
            upper = jnp.where(lane < half, both[:half, :LANES], both[half:FACET, :LANES])
            coeffs = jnp.concatenate([upper, both[FACET:, LANES:]], axis=0)
            fetches[ch].wait()
            dual = wave[ch] + coeffs
            out_ref[ch] = dual
            band = band_ref[ch]
            squares[band] = squares[band] + dual * dual
    share = height - taken_rows
    for source in range(copies):
        band, first = divmod(source * share, FACET)
        sums_ref[source, taken_rows:, :] = squares[band, first : first + share, :]


def weigh_kernel(me_ref, thresh_ref, weight_ref, parts_ref, out_ref, *, per, copies):
    for k in range(per):
        rows = pl.ds(k * FACET, FACET)
        total = parts_ref[0, rows]
        for source in range(1, copies):
            total = total + parts_ref[source, rows]
        threshold = thresh_ref[me_ref[0] * per + k]
        singular = jnp.sqrt(jnp.sum(total * total, keepdims=True))
        scaled = total * (1.0 - threshold / jnp.maximum(singular, threshold))
        for target in range(copies):
            out_ref[target, rows] = scaled
    total = parts_ref[0, per * FACET :]
    for source in range(1, copies):
        total = total + parts_ref[source, per * FACET :]
    weight = weight_ref[me_ref[0]]
    ratio = weight / jnp.maximum(jnp.sqrt(total), weight)
    for target in range(copies):
        out_ref[target, per * FACET :] = ratio


def finish_kernel(
    band_ref, basis_ref, combined_ref, dual_ref, all_ref, wave_ref, nuc_ref, wave, nuc, sems,
    *, chans, rank, per,
):
    share = all_ref.shape[1] - per * FACET
    pieces = FACET // share
    size = min(share, 32)
    copies = []
    for step, part in enumerate(range(0, FACET, size)):
        rows = pl.ds(part, size)
        scaled = [all_ref[k // per, pl.ds(k % per * FACET + part, size), :] for k in range(rank)]
        for ch in range(chans):
            total = basis_ref[0, ch] * scaled[0]
            for k in range(1, rank):
                total = total + basis_ref[k, ch] * scaled[k]
            nuc[ch, rows, :] = combined_ref[ch, rows, :] - total
            source = band_ref[ch] * pieces + part // share
            ratio = all_ref[source, pl.ds(per * FACET + part % share, size), :]
            wave[ch, rows, :] = dual_ref[ch, rows, :] * ratio
        for place, (held, out) in enumerate(((nuc, nuc_ref), (wave, wave_ref))):
            copy = pltpu.make_async_copy(held.at[:, rows, :], out.at[:, rows, :], sems.at[place, step])
            copy.start()
            copies.append(copy)
    for copy in copies:
        copy.wait()


def call(kernel, name, ins, outs, operands, scratch=(), flops=0, limit=24, places=None):
    size = sum(4 * int(np.prod(o.shape)) for o in outs) + sum(4 * int(np.prod(o.shape)) for o in operands)
    return pl.pallas_call(
        kernel,
        name=name,
        in_specs=ins,
        out_specs=places or [VMEM] * len(outs),
        out_shape=outs,
        scratch_shapes=list(scratch),
        compiler_params=pltpu.CompilerParams(vmem_limit_bytes=limit * 1024 * 1024),
        cost_estimate=pl.CostEstimate(flops=flops, bytes_accessed=size, transcendentals=0),
    )(*operands)


def f32(*shape):
    return jax.ShapeDtypeStruct(shape, jnp.float32)


def bf16(*shape):
    return jax.ShapeDtypeStruct(shape, jnp.bfloat16)


def shards(primal_slab, wave_dual, nuc_dual, l21_weights, nuc_thresh, basis, band_of, margin_width):
    chans = wave_dual.shape[0]
    spec, rows, cols = (lax.axis_size(a) for a in ("spec", "frow", "fcol"))
    senders = rows * cols
    deal = primal_slab.shape[1] // rows
    rank = basis.shape[3]
    bands = l21_weights.shape[0]
    plane = ("frow", "fcol")
    me = lax.axis_index("spec").astype(jnp.int32).reshape(1)
    local_basis = basis.reshape(chans, rank).T
    bands_here = band_of.reshape(chans)
    widths = margin_width.reshape(2)

    groups = chans // SLOTS
    block = deal * (chans + groups)
    (packed,) = call(
        functools.partial(pack_kernel, chans=chans, facet_rows=rows, facet_cols=cols, deal=deal),
        "pack", [VMEM], [f32(senders * block, LANES)],
        [primal_slab.reshape(-1, LANES)],
    )
    arrived = lax.all_to_all(
        packed.reshape(senders, block, LANES), plane, split_axis=0, concat_axis=0, tiled=True
    )
    centre, sides = column_operators()
    vertical, across = call(
        prepare_kernel, "prepare", [SMEM, VMEM, VMEM, VMEM],
        [bf16(3 * FACET // 2, 6 * LANES), bf16(SLOTS, 6 * LANES, 2 * LANES)],
        [widths, jnp.asarray(row_operator()), jnp.asarray(centre), jnp.asarray(sides)],
        scratch=[pltpu.VMEM((LANES, 2 * LANES), jnp.float32)],
    )
    strip = f32(chans + groups, EDGE, LANES)
    facet, side, top, bottom = call(
        functools.partial(unpack_kernel, chans=chans, deal=deal, senders=senders),
        "unpack", [VMEM],
        [f32(chans, FACET, LANES), f32(groups, FACET, LANES), strip, strip],
        [arrived.reshape(-1, LANES)],
    )
    above = lax.ppermute(bottom, "frow", [(i, i + 1) for i in range(rows - 1)])
    below = lax.ppermute(top, "frow", [(i + 1, i) for i in range(rows - 1)])
    combined, partial = call(
        functools.partial(project_kernel, chans=chans, rank=rank),
        "project", [VMEM, VMEM, SMEM],
        [f32(chans, FACET, LANES), f32(rank, FACET, LANES)],
        [facet, nuc_dual, local_basis],
        flops=2 * chans * rank * FACET * LANES,
    )
    per = rank // spec
    share = bands * FACET // spec
    dual_sum, sums = call(
        functools.partial(wavelet_kernel, chans=chans),
        "wavelet", [SMEM] + [VMEM] * 7 + [ANY],
        [f32(chans, FACET, LANES), f32(spec, per * FACET + share, LANES)],
        [bands_here, facet, side, above, below, vertical, across,
         partial.reshape(spec, per * FACET, LANES), wave_dual],
        scratch=[
            pltpu.VMEM((chans, FACET, LANES), jnp.float32),
            pltpu.VMEM((bands, FACET, LANES), jnp.float32),
            pltpu.SemaphoreType.DMA((chans,)),
        ],
        flops=2 * chans * 3 * 192 * 256 * 600,
    )
    parts = lax.all_to_all(sums, "spec", split_axis=0, concat_axis=0, tiled=True)
    (weighed,) = call(
        functools.partial(weigh_kernel, per=per, copies=spec),
        "weigh", [SMEM, SMEM, VMEM, VMEM], [f32(spec, per * FACET + share, LANES)],
        [me, nuc_thresh.reshape(rank), l21_weights.reshape(spec, share, LANES), parts],
    )
    everyone = lax.all_to_all(weighed, "spec", split_axis=0, concat_axis=0, tiled=True)
    wave_new, nuc_new = call(
        functools.partial(finish_kernel, chans=chans, rank=rank, per=per),
        "finish", [SMEM, SMEM, VMEM, VMEM, VMEM],
        [f32(chans, FACET, LANES), f32(chans, FACET, LANES)],
        [bands_here, local_basis, combined, dual_sum, everyone],
        scratch=[
            pltpu.VMEM((chans, FACET, LANES), jnp.float32),
            pltpu.VMEM((chans, FACET, LANES), jnp.float32),
            pltpu.SemaphoreType.DMA((2, FACET // min(share, 32))),
        ],
        flops=2 * chans * rank * FACET * LANES,
        places=[ANY, ANY],
    )
    return (wave_new, nuc_new)


def solution(mesh):
    return jax.shard_map(
        shards,
        mesh=mesh,
        in_specs=(
            P("spec", None, "frow", "fcol", None),
            P("spec", "frow", "fcol"),
            P("spec", "frow", "fcol"),
            P(None, "frow", "fcol"),
            P("frow", "fcol", None),
            P("frow", "fcol", "spec", None),
            P("frow", "fcol", "spec"),
            P("frow", "fcol", None),
        ),
        out_specs=(P("spec", "frow", "fcol"), P("spec", "frow", "fcol")),
        check_vma=False,
    )
```

```python
import functools

import jax
import jax.numpy as jnp
import numpy as np
from jax import lax
from jax.experimental import pallas as pl
from jax.experimental.pallas import tpu as pltpu
from jax.sharding import PartitionSpec as P

HALO = 21
EDGE = 24
SLOTS = 3
LANES = 128
FACET = 128
EXT = FACET + 2 * EDGE
VMEM = pl.BlockSpec(memory_space=pltpu.VMEM)
SMEM = pl.BlockSpec(memory_space=pltpu.SMEM)
HBM = pl.BlockSpec(memory_space=pltpu.HBM)

low_taps = [
    -0.00011747678400228192,
    0.0006754494059985568,
    -0.0003917403729959771,
    -0.00487035299301066,
    0.008746094047015655,
    0.013981027917015516,
    -0.04408825393106472,
    -0.01736930100202211,
    0.128747426620186,
    0.00047248457399797254,
    -0.2840155429624281,
    -0.015829105256023893,
    0.5853546836548691,
    0.6756307362980128,
    0.3128715909144659,
    0.05441584224308161,
]
tap_lag = 7
high_taps = [(-1.0) ** place * low_taps[15 - place] for place in range(16)]


def filter_matrix(in_length, taps, first, count):
    matrix = np.zeros((count, in_length))
    for out in range(count):
        matrix[out, 2 * (out + first) : 2 * (out + first) + 16] = taps
    return matrix


@functools.cache
def operators():
    length = FACET + 2 * HALO
    half, quarter = FACET // 2, FACET // 4
    low_all = filter_matrix(length, low_taps, 0, half + 14)
    high = filter_matrix(length, high_taps, tap_lag, half)
    low = low_all[tap_lag : tap_lag + half]
    coarse = np.concatenate(
        [
            filter_matrix(half + 14, low_taps, 0, quarter) @ low_all,
            filter_matrix(half + 14, high_taps, 0, quarter) @ low_all,
        ]
    )
    return coarse, low, high


def row_operator():
    whole = np.concatenate(operators())
    placed = np.zeros((whole.shape[0], 2 * LANES), np.float32)
    placed[:, :FACET] = whole[:, HALO : HALO + FACET]
    placed[:, FACET + EDGE - HALO : FACET + EDGE] = whole[:, :HALO]
    placed[:, FACET + EDGE : FACET + EDGE + HALO] = whole[:, HALO + FACET :]
    return placed


def column_operators():
    coarse, low, high = operators()
    whole = np.concatenate([coarse, high, low, high]).T.astype(np.float32)
    sides = np.zeros((2, EDGE, 2 * LANES), np.float32)
    sides[0, :HALO] = whole[:HALO]
    sides[1, :HALO] = whole[HALO + FACET :]
    return whole[HALO : HALO + FACET], sides


def split(values):
    head = values.astype(jnp.bfloat16)
    return head, (values - head.astype(jnp.float32)).astype(jnp.bfloat16)


def pack_kernel(rows_ref, out_ref, *, chans, facet_rows, facet_cols, deal):
    block = deal * (chans + chans // SLOTS)
    per_chan = deal * facet_rows * facet_cols
    for i in range(facet_rows):
        for q in range(deal):
            for j in range(facet_cols):
                first = (deal * i + q) * facet_cols + j
                out_ref[pl.ds((i * facet_cols + j) * block + q * chans, chans), :] = rows_ref[
                    pl.ds(first, chans, stride=per_chan), :
                ]
    lane = lax.broadcasted_iota(jnp.int32, (per_chan, LANES), 1)
    column = lax.broadcasted_iota(jnp.int32, (per_chan, LANES), 0) % facet_cols
    for group in range(chans // SLOTS):
        left = jnp.zeros((per_chan, LANES), jnp.float32)
        right = jnp.zeros((per_chan, LANES), jnp.float32)
        on_left = lane < 0
        for slot in range(SLOTS):
            rows = rows_ref[pl.ds((group * SLOTS + slot) * per_chan, per_chan), :]
            start = 2 * HALO * slot
            here = (lane >= start) & (lane < start + HALO)
            on_left = on_left | here
            left = jnp.where(here, pltpu.roll(rows, (start + HALO) % LANES, 1), left)
            here = (lane >= start + HALO) & (lane < start + 2 * HALO)
            right = jnp.where(here, pltpu.roll(rows, start + HALO, 1), right)
        left = jnp.where(column > 0, pltpu.roll(left, 1, 0), 0.0)
        right = jnp.where(column < facet_cols - 1, pltpu.roll(right, per_chan - 1, 0), 0.0)
        sides = jnp.where(on_left, left, right)
        for i in range(facet_rows):
            for q in range(deal):
                first = (deal * i + q) * facet_cols
                place = i * facet_cols * block + deal * chans + q * (chans // SLOTS) + group
                out_ref[pl.ds(place, facet_cols, stride=block), :] = sides[first : first + facet_cols]


def prepare_kernel(width_ref, rows_ref, centre_ref, sides_ref, v_ref, w_ref, pad):
    lane = lax.broadcasted_iota(jnp.int32, rows_ref.shape, 1)
    up = (lane < FACET) | ((lane >= FACET + EDGE - width_ref[0]) & (lane < FACET + EDGE + width_ref[0]))
    head, tail = split(jnp.where(up, rows_ref[...], 0.0))
    v_ref[:, : 2 * LANES] = head
    v_ref[:, 2 * LANES : 4 * LANES] = tail
    v_ref[:, 4 * LANES :] = head
    place = lax.broadcasted_iota(jnp.int32, sides_ref.shape[1:], 0)
    before = jnp.where(place >= HALO - width_ref[1], sides_ref[0], 0.0)[:HALO]
    after = jnp.where(place < width_ref[1], sides_ref[1], 0.0)[:HALO]
    centre_head, centre_tail = split(centre_ref[...])
    for slot in range(SLOTS):
        pad[...] = jnp.zeros_like(pad)
        pad[2 * HALO * slot : 2 * HALO * slot + HALO, :] = before
        pad[2 * HALO * slot + HALO : 2 * HALO * (slot + 1), :] = after
        head, tail = split(pad[...])
        w_ref[slot] = jnp.concatenate(
            [centre_head, head, centre_head, head, centre_tail, tail], axis=0
        )


def unpack_kernel(in_ref, facet_ref, side_ref, top_ref, bottom_ref, *, chans, deal, senders):
    groups = chans // SLOTS
    block = deal * (chans + groups)
    for at in range(chans + groups):
        if at < chans:
            starts = [q * chans + at for q in range(deal)]
        else:
            starts = [deal * chans + q * groups + at - chans for q in range(deal)]
        rows = jnp.concatenate([in_ref[pl.ds(s, senders, stride=block), :] for s in starts], axis=0)
        if at < chans:
            facet_ref[at] = rows
        else:
            side_ref[at - chans] = rows
        top_ref[at] = rows[:EDGE]
        bottom_ref[at] = rows[FACET - EDGE :]


def project_kernel(facet_ref, nuc_ref, basis_ref, combined_ref, out_ref, *, chans, rank):
    for part in range(0, FACET, 32):
        rows = pl.ds(part, 32)
        total = [None] * rank
        for ch in range(chans):
            block = nuc_ref[ch, rows, :] + facet_ref[ch, rows, :]
            combined_ref[ch, rows, :] = block
            for k in range(rank):
                term = basis_ref[k, ch] * block
                total[k] = term if total[k] is None else total[k] + term
        for k in range(rank):
            out_ref[k, rows, :] = total[k]


def wavelet_kernel(
    me_ref, band_ref, facet_ref, side_ref, above_ref, below_ref, v_ref, w_ref, partial_ref, wave_ref,
    out_ref, own_ref, other_ref, wave, squares, sems, *, chans,
):
    fetches = [pltpu.make_async_copy(wave_ref.at[ch], wave.at[ch], sems.at[ch]) for ch in range(chans)]
    for fetch in fetches:
        fetch.start()
    core = me_ref[0] % 2
    chips = own_ref.shape[0]
    share = own_ref.shape[1] - FACET
    for chip in range(chips):
        own_ref[chip, :FACET, :] = partial_ref[2 * chip + core]
        other_ref[chip, :FACET, :] = partial_ref[2 * chip + 1 - core]
    squares[...] = jnp.zeros_like(squares)
    groups = chans // SLOTS
    half = FACET // 2
    lane = lax.broadcasted_iota(jnp.int32, (half, LANES), 1)
    nothing = jnp.zeros((2 * LANES - EXT, 2 * LANES), jnp.bfloat16)
    sides = [
        split(jnp.concatenate([side_ref[g], above_ref[chans + g], below_ref[chans + g]], axis=0))
        for g in range(groups)
    ]
    for slot in range(SLOTS):
        for group in range(groups):
            ch = group * SLOTS + slot
            rows = jnp.concatenate([facet_ref[ch], above_ref[ch], below_ref[ch]], axis=0)
            head, tail = split(rows)
            side_head, side_tail = sides[group]
            taken = jnp.concatenate([head, side_head, tail, side_tail, head, side_head], axis=1)
            across = jnp.dot(taken, w_ref[slot], preferred_element_type=jnp.float32)
            head, tail = split(across)
            stacked = jnp.concatenate([head, nothing, head, nothing, tail, nothing], axis=0)
            both = jnp.dot(v_ref[...], stacked, preferred_element_type=jnp.float32)
            upper = jnp.where(lane < half, both[:half, :LANES], both[half:FACET, :LANES])
            coeffs = jnp.concatenate([upper, both[FACET:, LANES:]], axis=0)
            fetches[ch].wait()
            dual = wave[ch] + coeffs
            out_ref[ch] = dual
            rows = pl.ds(pl.multiple_of(band_ref[ch] * FACET, FACET), FACET)
            squares[rows, :] = squares[rows, :] + dual * dual
    for chip in range(chips):
        first = pl.multiple_of((2 * chip + core) * share, share)
        own_ref[chip, FACET:, :] = squares[pl.ds(first, share), :]
        first = pl.multiple_of((2 * chip + 1 - core) * share, share)
        other_ref[chip, FACET:, :] = squares[pl.ds(first, share), :]


def pair_kernel(me_ref, own_ref, came_ref, *outs):
    chips = own_ref.shape[0]
    for step, out_ref in enumerate(outs):
        chip = (me_ref[0] // 2 + step) % chips
        out_ref[...] = own_ref[chip] + came_ref[chip]


def weigh_kernel(me_ref, thresh_ref, weight_ref, *refs):
    parts, out_ref = refs[:-1], refs[-1]
    total = parts[0][...]
    for part in parts[1:]:
        total = total + part[...]
    spectrum, squares = total[:FACET], total[FACET:]
    threshold = thresh_ref[me_ref[0]]
    singular = jnp.sqrt(jnp.sum(spectrum * spectrum, keepdims=True))
    out_ref[:FACET] = spectrum * (1.0 - threshold / jnp.maximum(singular, threshold))
    weight = weight_ref[me_ref[0]]
    out_ref[FACET:] = weight / jnp.maximum(jnp.sqrt(squares), weight)


def stack_kernel(*refs):
    for place, ref in enumerate(refs[:-1]):
        refs[-1][place] = ref[...]


def finish_kernel(
    me_ref, band_ref, basis_ref, combined_ref, dual_ref, own_ref, other_ref, wave_ref, nuc_ref,
    ordered, wave, nuc, sems, *, chans, rank,
):
    core, chips = me_ref[0] % 2, own_ref.shape[0]
    for step in range(chips):
        chip = (me_ref[0] // 2 + chips - step) % chips
        ordered[2 * chip + core] = own_ref[step]
        ordered[2 * chip + 1 - core] = other_ref[step]
    share = ordered.shape[1] - FACET
    pieces = FACET // share
    copies = []
    for part in range(pieces):
        rows = pl.ds(part * share, share)
        scaled = [ordered[k, rows, :] for k in range(rank)]
        for ch in range(chans):
            total = basis_ref[0, ch] * scaled[0]
            for k in range(1, rank):
                total = total + basis_ref[k, ch] * scaled[k]
            nuc[ch, rows, :] = combined_ref[ch, rows, :] - total
            ratio = ordered[band_ref[ch] * pieces + part, FACET:, :]
            wave[ch, rows, :] = dual_ref[ch, rows, :] * ratio
        for place, (held, out) in enumerate(((nuc, nuc_ref), (wave, wave_ref))):
            copy = pltpu.make_async_copy(held.at[:, rows, :], out.at[:, rows, :], sems.at[place, part])
            copy.start()
            copies.append(copy)
    for copy in copies:
        copy.wait()


def call(kernel, name, ins, outs, operands, scratch=(), flops=0, limit=24, places=None):
    size = sum(4 * int(np.prod(o.shape)) for o in outs) + sum(4 * int(np.prod(o.shape)) for o in operands)
    return pl.pallas_call(
        kernel,
        name=name,
        in_specs=ins,
        out_specs=places or [VMEM] * len(outs),
        out_shape=outs,
        scratch_shapes=list(scratch),
        compiler_params=pltpu.CompilerParams(vmem_limit_bytes=limit * 1024 * 1024),
        cost_estimate=pl.CostEstimate(flops=flops, bytes_accessed=size, transcendentals=0),
    )(*operands)


def f32(*shape):
    return jax.ShapeDtypeStruct(shape, jnp.float32)


def bf16(*shape):
    return jax.ShapeDtypeStruct(shape, jnp.bfloat16)


def shards(primal_slab, wave_dual, nuc_dual, l21_weights, nuc_thresh, basis, band_of, margin_width):
    chans = wave_dual.shape[0]
    spec, rows, cols = (lax.axis_size(a) for a in ("spec", "frow", "fcol"))
    senders = rows * cols
    deal = primal_slab.shape[1] // rows
    rank = basis.shape[3]
    bands = l21_weights.shape[0]
    plane = ("frow", "fcol")
    me = lax.axis_index("spec").astype(jnp.int32).reshape(1)
    local_basis = basis.reshape(chans, rank).T
    bands_here = band_of.reshape(chans)
    widths = margin_width.reshape(2)

    groups = chans // SLOTS
    block = deal * (chans + groups)
    (packed,) = call(
        functools.partial(pack_kernel, chans=chans, facet_rows=rows, facet_cols=cols, deal=deal),
        "pack", [VMEM], [f32(senders * block, LANES)],
        [primal_slab.reshape(-1, LANES)],
    )
    arrived = lax.all_to_all(
        packed.reshape(senders, block, LANES), plane, split_axis=0, concat_axis=0, tiled=True
    )
    centre, sides = column_operators()
    vertical, across = call(
        prepare_kernel, "prepare", [SMEM, VMEM, VMEM, VMEM],
        [bf16(3 * FACET // 2, 6 * LANES), bf16(SLOTS, 6 * LANES, 2 * LANES)],
        [widths, jnp.asarray(row_operator()), jnp.asarray(centre), jnp.asarray(sides)],
        scratch=[pltpu.VMEM((LANES, 2 * LANES), jnp.float32)],
    )
    strip = f32(chans + groups, EDGE, LANES)
    facet, side, top, bottom = call(
        functools.partial(unpack_kernel, chans=chans, deal=deal, senders=senders),
        "unpack", [VMEM],
        [f32(chans, FACET, LANES), f32(groups, FACET, LANES), strip, strip],
        [arrived.reshape(-1, LANES)],
    )
    above = lax.ppermute(bottom, "frow", [(i, i + 1) for i in range(rows - 1)])
    below = lax.ppermute(top, "frow", [(i + 1, i) for i in range(rows - 1)])
    combined, partial = call(
        functools.partial(project_kernel, chans=chans, rank=rank),
        "project", [VMEM, VMEM, SMEM],
        [f32(chans, FACET, LANES), f32(rank, FACET, LANES)],
        [facet, nuc_dual, local_basis],
        flops=2 * chans * rank * FACET * LANES,
    )
    share = bands * FACET // spec
    chips = spec // 2
    chunk, chunks = f32(FACET + share, LANES), f32(chips, FACET + share, LANES)
    dual_sum, own, other = call(
        functools.partial(wavelet_kernel, chans=chans),
        "wavelet", [SMEM, SMEM] + [VMEM] * 7 + [HBM],
        [f32(chans, FACET, LANES), chunks, chunks],
        [me, bands_here, facet, side, above, below, vertical, across, partial, wave_dual],
        scratch=[
            pltpu.VMEM((chans, FACET, LANES), jnp.float32),
            pltpu.VMEM((bands * FACET, LANES), jnp.float32),
            pltpu.SemaphoreType.DMA((chans,)),
        ],
        flops=2 * chans * 3 * 192 * 256 * 600,
    )

    def swap(values):
        return lax.ppermute(values, "spec", [(i, i ^ 1) for i in range(spec)])

    def onward(values, step):
        return lax.ppermute(values, "spec", [(i, (i + 2 * step) % spec) for i in range(spec)])

    steps = range(1, chips)
    mine = call(pair_kernel, "pair", [SMEM, VMEM, VMEM], [chunk] * chips, [me, own, swap(other)])
    came = [onward(mine[step], step) for step in steps]
    (weighed,) = call(
        weigh_kernel, "weigh", [SMEM, SMEM, VMEM] + [VMEM] * chips, [chunk],
        [me, nuc_thresh.reshape(rank), l21_weights.reshape(spec, share, LANES), mine[0], *came],
    )
    gathered = [weighed] + [onward(weighed, step) for step in steps]
    (stacked,) = call(stack_kernel, "stack", [VMEM] * chips, [chunks], gathered)
    wave_new, nuc_new = call(
        functools.partial(finish_kernel, chans=chans, rank=rank),
        "finish", [SMEM, SMEM, SMEM] + [VMEM] * 4,
        [f32(chans, FACET, LANES), f32(chans, FACET, LANES)],
        [me, bands_here, local_basis, combined, dual_sum, stacked, swap(stacked)],
        scratch=[
            pltpu.VMEM((spec, FACET + share, LANES), jnp.float32),
            pltpu.VMEM((chans, FACET, LANES), jnp.float32),
            pltpu.VMEM((chans, FACET, LANES), jnp.float32),
            pltpu.SemaphoreType.DMA((2, FACET // share)),
        ],
        flops=2 * chans * rank * FACET * LANES,
        places=[HBM, HBM],
    )
    return (wave_new, nuc_new)


def solution(mesh):
    return jax.shard_map(
        shards,
        mesh=mesh,
        in_specs=(
            P("spec", None, "frow", "fcol", None),
            P("spec", "frow", "fcol"),
            P("spec", "frow", "fcol"),
            P(None, "frow", "fcol"),
            P("frow", "fcol", None),
            P("frow", "fcol", "spec", None),
            P("frow", "fcol", "spec"),
            P("frow", "fcol", None),
        ),
        out_specs=(P("spec", "frow", "fcol"), P("spec", "frow", "fcol")),
        check_vma=False,
    )
```

```python
import functools

import jax
import jax.numpy as jnp
import numpy as np
from jax import lax
from jax.experimental import pallas as pl
from jax.experimental.pallas import tpu as pltpu
from jax.sharding import PartitionSpec as P

HALO = 21
EDGE = 24
SLOTS = 3
LANES = 128
FACET = 128
EXT = FACET + 2 * EDGE
VMEM = pl.BlockSpec(memory_space=pltpu.VMEM)
SMEM = pl.BlockSpec(memory_space=pltpu.SMEM)
HBM = pl.BlockSpec(memory_space=pltpu.HBM)

low_taps = [
    -0.00011747678400228192,
    0.0006754494059985568,
    -0.0003917403729959771,
    -0.00487035299301066,
    0.008746094047015655,
    0.013981027917015516,
    -0.04408825393106472,
    -0.01736930100202211,
    0.128747426620186,
    0.00047248457399797254,
    -0.2840155429624281,
    -0.015829105256023893,
    0.5853546836548691,
    0.6756307362980128,
    0.3128715909144659,
    0.05441584224308161,
]
tap_lag = 7
high_taps = [(-1.0) ** place * low_taps[15 - place] for place in range(16)]


def filter_matrix(in_length, taps, first, count):
    matrix = np.zeros((count, in_length))
    for out in range(count):
        matrix[out, 2 * (out + first) : 2 * (out + first) + 16] = taps
    return matrix


@functools.cache
def operators():
    length = FACET + 2 * HALO
    half, quarter = FACET // 2, FACET // 4
    low_all = filter_matrix(length, low_taps, 0, half + 14)
    high = filter_matrix(length, high_taps, tap_lag, half)
    low = low_all[tap_lag : tap_lag + half]
    coarse = np.concatenate(
        [
            filter_matrix(half + 14, low_taps, 0, quarter) @ low_all,
            filter_matrix(half + 14, high_taps, 0, quarter) @ low_all,
        ]
    )
    return coarse, low, high


def row_operator():
    whole = np.concatenate(operators())
    placed = np.zeros((2, whole.shape[0], 2 * LANES), np.float32)
    placed[:, :, :FACET] = whole[:, HALO : HALO + FACET]
    above, below = whole[:, :HALO], whole[:, HALO + FACET :]
    placed[0, :, FACET : FACET + HALO] = below
    placed[0, :, EXT - HALO : EXT] = above
    placed[1, :, FACET + EDGE - HALO : FACET + EDGE] = above
    placed[1, :, FACET + EDGE : FACET + EDGE + HALO] = below
    return placed


def column_operators():
    coarse, low, high = operators()
    whole = np.concatenate([coarse, high, low, high]).T.astype(np.float32)
    sides = np.zeros((2, EDGE, 2 * LANES), np.float32)
    sides[0, :HALO] = whole[:HALO]
    sides[1, :HALO] = whole[HALO + FACET :]
    return whole[HALO : HALO + FACET], sides


def split(values):
    head = values.astype(jnp.bfloat16)
    return head, (values - head.astype(jnp.float32)).astype(jnp.bfloat16)


def pack_kernel(rows_ref, out_ref, *, chans, facet_rows, facet_cols, deal):
    block = deal * (chans + chans // SLOTS)
    per_chan = deal * facet_rows * facet_cols
    for i in range(facet_rows):
        for q in range(deal):
            for j in range(facet_cols):
                first = (deal * i + q) * facet_cols + j
                out_ref[pl.ds((i * facet_cols + j) * block + q * chans, chans), :] = rows_ref[
                    pl.ds(first, chans, stride=per_chan), :
                ]
    lane = lax.broadcasted_iota(jnp.int32, (per_chan, LANES), 1)
    column = lax.broadcasted_iota(jnp.int32, (per_chan, LANES), 0) % facet_cols
    for group in range(chans // SLOTS):
        left = jnp.zeros((per_chan, LANES), jnp.float32)
        right = jnp.zeros((per_chan, LANES), jnp.float32)
        on_left = lane < 0
        for slot in range(SLOTS):
            rows = rows_ref[pl.ds((group * SLOTS + slot) * per_chan, per_chan), :]
            start = 2 * HALO * slot
            here = (lane >= start) & (lane < start + HALO)
            on_left = on_left | here
            left = jnp.where(here, pltpu.roll(rows, (start + HALO) % LANES, 1), left)
            here = (lane >= start + HALO) & (lane < start + 2 * HALO)
            right = jnp.where(here, pltpu.roll(rows, start + HALO, 1), right)
        left = jnp.where(column > 0, pltpu.roll(left, 1, 0), 0.0)
        right = jnp.where(column < facet_cols - 1, pltpu.roll(right, per_chan - 1, 0), 0.0)
        sides = jnp.where(on_left, left, right)
        for i in range(facet_rows):
            for q in range(deal):
                first = (deal * i + q) * facet_cols
                place = i * facet_cols * block + deal * chans + q * (chans // SLOTS) + group
                out_ref[pl.ds(place, facet_cols, stride=block), :] = sides[first : first + facet_cols]


def prepare_kernel(me_ref, width_ref, rows_ref, centre_ref, sides_ref, v_ref, w_ref, pad):
    odd = me_ref[1] % 2
    lane = lax.broadcasted_iota(jnp.int32, rows_ref.shape[1:], 1)
    first = jnp.where(odd == 1, FACET + EDGE - width_ref[0], EXT - width_ref[0])
    last = jnp.where(odd == 1, FACET + EDGE, FACET) + width_ref[0]
    above = (lane >= first) & (lane < first + width_ref[0])
    below = (lane >= last - width_ref[0]) & (lane < last)
    head, tail = split(jnp.where((lane < FACET) | above | below, rows_ref[odd], 0.0))
    v_ref[:, : 2 * LANES] = head
    v_ref[:, 2 * LANES : 4 * LANES] = tail
    v_ref[:, 4 * LANES :] = head
    place = lax.broadcasted_iota(jnp.int32, sides_ref.shape[1:], 0)
    before = jnp.where(place >= HALO - width_ref[1], sides_ref[0], 0.0)[:HALO]
    after = jnp.where(place < width_ref[1], sides_ref[1], 0.0)[:HALO]
    centre_head, centre_tail = split(centre_ref[...])
    for slot in range(SLOTS):
        pad[...] = jnp.zeros_like(pad)
        pad[2 * HALO * slot : 2 * HALO * slot + HALO, :] = before
        pad[2 * HALO * slot + HALO : 2 * HALO * (slot + 1), :] = after
        head, tail = split(pad[...])
        w_ref[slot] = jnp.concatenate(
            [centre_head, head, centre_head, head, centre_tail, tail], axis=0
        )


def unpack_kernel(me_ref, in_ref, facet_ref, side_ref, first_ref, second_ref, *, chans, deal, senders):
    groups = chans // SLOTS
    block = deal * (chans + groups)
    odd = me_ref[1] % 2
    first = pl.ds(pl.multiple_of((FACET - EDGE) * (1 - odd), 8), EDGE)
    second = pl.ds(pl.multiple_of((FACET - EDGE) * odd, 8), EDGE)
    for at in range(chans + groups):
        if at < chans:
            starts = [q * chans + at for q in range(deal)]
        else:
            starts = [deal * chans + q * groups + at - chans for q in range(deal)]
        rows = jnp.concatenate([in_ref[pl.ds(s, senders, stride=block), :] for s in starts], axis=0)
        held, place = (facet_ref, at) if at < chans else (side_ref, at - chans)
        held[place] = rows
        first_ref[at] = held[place, first, :]
        second_ref[at] = held[place, second, :]


def project_kernel(facet_ref, nuc_ref, basis_ref, combined_ref, out_ref, *, chans, rank):
    for part in range(0, FACET, 32):
        rows = pl.ds(part, 32)
        total = [None] * rank
        for ch in range(chans):
            block = nuc_ref[ch, rows, :] + facet_ref[ch, rows, :]
            combined_ref[ch, rows, :] = block
            for k in range(rank):
                term = basis_ref[k, ch] * block
                total[k] = term if total[k] is None else total[k] + term
        for k in range(rank):
            out_ref[k, rows, :] = total[k]


def wavelet_kernel(
    me_ref, band_ref, facet_ref, side_ref, first_ref, second_ref, v_ref, w_ref, partial_ref, wave_ref,
    out_ref, own_ref, other_ref, squares, *, chans,
):
    core = me_ref[0] % 2
    chips = own_ref.shape[0]
    share = own_ref.shape[1] - FACET
    for chip in range(chips):
        own_ref[chip, :FACET, :] = partial_ref[2 * chip + core]
        other_ref[chip, :FACET, :] = partial_ref[2 * chip + 1 - core]
    squares[...] = jnp.zeros_like(squares)
    groups = chans // SLOTS
    half = FACET // 2
    lane = lax.broadcasted_iota(jnp.int32, (half, LANES), 1)
    nothing = jnp.zeros((2 * LANES - EXT, 2 * LANES), jnp.bfloat16)
    sides = [
        split(jnp.concatenate([side_ref[g], first_ref[chans + g], second_ref[chans + g]], axis=0))
        for g in range(groups)
    ]
    for slot in range(SLOTS):
        for group in range(groups):
            ch = group * SLOTS + slot
            rows = jnp.concatenate([facet_ref[ch], first_ref[ch], second_ref[ch]], axis=0)
            head, tail = split(rows)
            side_head, side_tail = sides[group]
            taken = jnp.concatenate([head, side_head, tail, side_tail, head, side_head], axis=1)
            across = jnp.dot(taken, w_ref[slot], preferred_element_type=jnp.float32)
            head, tail = split(across)
            stacked = jnp.concatenate([head, nothing, head, nothing, tail, nothing], axis=0)
            both = jnp.dot(v_ref[...], stacked, preferred_element_type=jnp.float32)
            upper = jnp.where(lane < half, both[:half, :LANES], both[half:FACET, :LANES])
            coeffs = jnp.concatenate([upper, both[FACET:, LANES:]], axis=0)
            dual = wave_ref[ch] + coeffs
            out_ref[ch] = dual
            rows = pl.ds(pl.multiple_of(band_ref[ch] * FACET, FACET), FACET)
            squares[rows, :] = squares[rows, :] + dual * dual
    for chip in range(chips):
        first = pl.multiple_of((2 * chip + core) * share, share)
        own_ref[chip, FACET:, :] = squares[pl.ds(first, share), :]
        first = pl.multiple_of((2 * chip + 1 - core) * share, share)
        other_ref[chip, FACET:, :] = squares[pl.ds(first, share), :]


def pair_kernel(own_ref, came_ref, out_ref):
    out_ref[...] = own_ref[...] + came_ref[...]


def weigh_kernel(me_ref, thresh_ref, weight_ref, parts_ref, out_ref):
    chips = parts_ref.shape[0]
    total = parts_ref[0]
    for chip in range(1, chips):
        total = total + parts_ref[chip]
    spectrum, squares = total[:FACET], total[FACET:]
    threshold = thresh_ref[me_ref[0]]
    singular = jnp.sqrt(jnp.sum(spectrum * spectrum, keepdims=True))
    scaled = spectrum * (1.0 - threshold / jnp.maximum(singular, threshold))
    weight = weight_ref[me_ref[0]]
    ratio = weight / jnp.maximum(jnp.sqrt(squares), weight)
    for chip in range(chips):
        out_ref[chip, :FACET] = scaled
        out_ref[chip, FACET:] = ratio


def finish_kernel(
    me_ref, band_ref, basis_ref, combined_ref, dual_ref, own_ref, other_ref, wave_ref, nuc_ref,
    ordered, wave, nuc, sems, *, chans, rank,
):
    core, chips = me_ref[0] % 2, own_ref.shape[0]
    for chip in range(chips):
        ordered[2 * chip + core] = own_ref[chip]
        ordered[2 * chip + 1 - core] = other_ref[chip]
    share = ordered.shape[1] - FACET
    pieces = FACET // share
    copies = []
    for part in range(pieces):
        rows = pl.ds(part * share, share)
        scaled = [ordered[k, rows, :] for k in range(rank)]
        for ch in range(chans):
            total = basis_ref[0, ch] * scaled[0]
            for k in range(1, rank):
                total = total + basis_ref[k, ch] * scaled[k]
            nuc[ch, rows, :] = combined_ref[ch, rows, :] - total
            ratio = ordered[band_ref[ch] * pieces + part, FACET:, :]
            wave[ch, rows, :] = dual_ref[ch, rows, :] * ratio
        for place, (held, out) in enumerate(((nuc, nuc_ref), (wave, wave_ref))):
            copy = pltpu.make_async_copy(held.at[:, rows, :], out.at[:, rows, :], sems.at[place, part])
            copy.start()
            copies.append(copy)
    for copy in copies:
        copy.wait()


def call(kernel, name, ins, outs, operands, scratch=(), flops=0, limit=24, places=None):
    size = sum(4 * int(np.prod(o.shape)) for o in outs) + sum(4 * int(np.prod(o.shape)) for o in operands)
    return pl.pallas_call(
        kernel,
        name=name,
        in_specs=ins,
        out_specs=places or [VMEM] * len(outs),
        out_shape=outs,
        scratch_shapes=list(scratch),
        compiler_params=pltpu.CompilerParams(vmem_limit_bytes=limit * 1024 * 1024),
        cost_estimate=pl.CostEstimate(flops=flops, bytes_accessed=size, transcendentals=0),
    )(*operands)


def f32(*shape):
    return jax.ShapeDtypeStruct(shape, jnp.float32)


def bf16(*shape):
    return jax.ShapeDtypeStruct(shape, jnp.bfloat16)


def shards(primal_slab, wave_dual, nuc_dual, l21_weights, nuc_thresh, basis, band_of, margin_width):
    chans = wave_dual.shape[0]
    spec, rows, cols = (lax.axis_size(a) for a in ("spec", "frow", "fcol"))
    senders = rows * cols
    deal = primal_slab.shape[1] // rows
    rank = basis.shape[3]
    bands = l21_weights.shape[0]
    plane = ("frow", "fcol")
    me = jnp.stack([lax.axis_index("spec"), lax.axis_index("frow")]).astype(jnp.int32)
    local_basis = basis.reshape(chans, rank).T
    bands_here = band_of.reshape(chans)
    widths = margin_width.reshape(2)

    groups = chans // SLOTS
    block = deal * (chans + groups)
    (packed,) = call(
        functools.partial(pack_kernel, chans=chans, facet_rows=rows, facet_cols=cols, deal=deal),
        "pack", [VMEM], [f32(senders * block, LANES)],
        [primal_slab.reshape(-1, LANES)],
    )
    arrived = lax.all_to_all(
        packed.reshape(senders, block, LANES), plane, split_axis=0, concat_axis=0, tiled=True
    )
    centre, sides = column_operators()
    vertical, across = call(
        prepare_kernel, "prepare", [SMEM, SMEM, VMEM, VMEM, VMEM],
        [bf16(3 * FACET // 2, 6 * LANES), bf16(SLOTS, 6 * LANES, 2 * LANES)],
        [me, widths, jnp.asarray(row_operator()), jnp.asarray(centre), jnp.asarray(sides)],
        scratch=[pltpu.VMEM((LANES, 2 * LANES), jnp.float32)],
    )
    strip = f32(chans + groups, EDGE, LANES)
    facet, side, first, second = call(
        functools.partial(unpack_kernel, chans=chans, deal=deal, senders=senders),
        "unpack", [SMEM, VMEM],
        [f32(chans, FACET, LANES), f32(groups, FACET, LANES), strip, strip],
        [me, arrived.reshape(-1, LANES)],
    )
    first = lax.ppermute(first, "frow", [(i, i ^ 1) for i in range(rows)])
    other = [(i, i - 1 if i % 2 == 0 else i + 1) for i in range(1, rows - 1)]
    second = lax.ppermute(second, "frow", other)
    combined, partial = call(
        functools.partial(project_kernel, chans=chans, rank=rank),
        "project", [VMEM, VMEM, SMEM],
        [f32(chans, FACET, LANES), f32(rank, FACET, LANES)],
        [facet, nuc_dual, local_basis],
        flops=2 * chans * rank * FACET * LANES,
    )
    share = bands * FACET // spec
    chips = spec // 2
    chunks = f32(chips, FACET + share, LANES)
    dual_sum, own, other = call(
        functools.partial(wavelet_kernel, chans=chans),
        "wavelet", [SMEM, SMEM] + [VMEM] * 8,
        [f32(chans, FACET, LANES), chunks, chunks],
        [me, bands_here, facet, side, first, second, vertical, across, partial, wave_dual],
        scratch=[
            pltpu.VMEM((bands * FACET, LANES), jnp.float32),
        ],
        flops=2 * chans * 3 * 192 * 256 * 600,
    )

    def swap(values):
        return lax.ppermute(values, "spec", [(i, i ^ 1) for i in range(spec)])

    def across_chips(values):
        cores = [list(range(core, spec, 2)) for core in range(2)]
        return lax.all_to_all(
            values, "spec", split_axis=0, concat_axis=0, tiled=True, axis_index_groups=cores
        )

    (sums,) = call(pair_kernel, "pair", [VMEM, VMEM], [chunks], [own, swap(other)])
    (weighed,) = call(
        weigh_kernel, "weigh", [SMEM, SMEM, VMEM, VMEM], [chunks],
        [me, nuc_thresh.reshape(rank), l21_weights.reshape(spec, share, LANES), across_chips(sums)],
    )
    own = across_chips(weighed)
    wave_new, nuc_new = call(
        functools.partial(finish_kernel, chans=chans, rank=rank),
        "finish", [SMEM, SMEM, SMEM] + [VMEM] * 4,
        [f32(chans, FACET, LANES), f32(chans, FACET, LANES)],
        [me, bands_here, local_basis, combined, dual_sum, own, swap(own)],
        scratch=[
            pltpu.VMEM((spec, FACET + share, LANES), jnp.float32),
            pltpu.VMEM((chans, FACET, LANES), jnp.float32),
            pltpu.VMEM((chans, FACET, LANES), jnp.float32),
            pltpu.SemaphoreType.DMA((2, FACET // share)),
        ],
        flops=2 * chans * rank * FACET * LANES,
        places=[HBM, HBM],
    )
    return (wave_new, nuc_new)


def solution(mesh):
    return jax.shard_map(
        shards,
        mesh=mesh,
        in_specs=(
            P("spec", None, "frow", "fcol", None),
            P("spec", "frow", "fcol"),
            P("spec", "frow", "fcol"),
            P(None, "frow", "fcol"),
            P("frow", "fcol", None),
            P("frow", "fcol", "spec", None),
            P("frow", "fcol", "spec"),
            P("frow", "fcol", None),
        ),
        out_specs=(P("spec", "frow", "fcol"), P("spec", "frow", "fcol")),
        check_vma=False,
    )
```

```python
import functools

import jax
import jax.numpy as jnp
import numpy as np
from jax import lax
from jax.experimental import pallas as pl
from jax.experimental.pallas import tpu as pltpu
from jax.sharding import PartitionSpec as P

HALO = 21
EDGE = 24
SLOTS = 3
LANES = 128
FACET = 128
HALF = FACET // 2
CUT = 40
EXT = HALF + 2 * EDGE
PIECES = (
    (0, 32, True, 0),
    (32, 8, True, 32),
    (40, 24, False, 40),
    (64, 32, False, 0),
    (96, 8, False, 32),
    (104, 24, True, 40),
)
VMEM = pl.BlockSpec(memory_space=pltpu.VMEM)
SMEM = pl.BlockSpec(memory_space=pltpu.SMEM)
HBM = pl.BlockSpec(memory_space=pltpu.HBM)

low_taps = [
    -0.00011747678400228192,
    0.0006754494059985568,
    -0.0003917403729959771,
    -0.00487035299301066,
    0.008746094047015655,
    0.013981027917015516,
    -0.04408825393106472,
    -0.01736930100202211,
    0.128747426620186,
    0.00047248457399797254,
    -0.2840155429624281,
    -0.015829105256023893,
    0.5853546836548691,
    0.6756307362980128,
    0.3128715909144659,
    0.05441584224308161,
]
tap_lag = 7
high_taps = [(-1.0) ** place * low_taps[15 - place] for place in range(16)]


def filter_matrix(in_length, taps, first, count):
    matrix = np.zeros((count, in_length))
    for out in range(count):
        matrix[out, 2 * (out + first) : 2 * (out + first) + 16] = taps
    return matrix


@functools.cache
def operators():
    length = FACET + 2 * HALO
    half, quarter = FACET // 2, FACET // 4
    low_all = filter_matrix(length, low_taps, 0, half + 14)
    high = filter_matrix(length, high_taps, tap_lag, half)
    low = low_all[tap_lag : tap_lag + half]
    coarse = np.concatenate(
        [
            filter_matrix(half + 14, low_taps, 0, quarter) @ low_all,
            filter_matrix(half + 14, high_taps, 0, quarter) @ low_all,
        ]
    )
    return coarse, low, high


def row_operators():
    whole = np.concatenate(operators()).astype(np.float32)
    above, facet, below = whole[:, :HALO], whole[:, HALO : HALO + FACET], whole[:, HALO + FACET :]
    outer = np.zeros((2, whole.shape[0], LANES), np.float32)
    outer[:, :, :HALF] = np.concatenate([facet[:, :CUT], facet[:, HALF + CUT :]], axis=1)
    outer[0, :, HALF : HALF + HALO] = below
    outer[0, :, HALF + 2 * EDGE - HALO : HALF + 2 * EDGE] = above
    outer[1, :, HALF + EDGE - HALO : HALF + EDGE] = above
    outer[1, :, HALF + EDGE : HALF + EDGE + HALO] = below
    inner = np.concatenate([facet[:, HALF : HALF + CUT], facet[:, CUT:HALF]], axis=1)
    return np.concatenate([outer] * 3, axis=2), np.concatenate([inner] * 3, axis=1)


def column_operators():
    coarse, low, high = operators()
    whole = np.concatenate([coarse, high, low, high]).T.astype(np.float32)
    sides = np.zeros((2, EDGE, 2 * LANES), np.float32)
    sides[0, :HALO] = whole[:HALO]
    sides[1, :HALO] = whole[HALO + FACET :]
    return whole[HALO : HALO + FACET], sides


def split(values):
    head = values.astype(jnp.bfloat16)
    return head, (values - head.astype(jnp.float32)).astype(jnp.bfloat16)


def pack_kernel(me_ref, rows_ref, outer_ref, inner_ref, *, chans, facet_rows, facet_cols):
    groups = chans // SLOTS
    block = chans + groups
    per_chan = 2 * facet_rows * facet_cols
    late = me_ref[1] * facet_cols >= CUT

    def store(i, first, size, stride, rows):
        place = pl.ds(i * facet_cols * block + first, size, stride=stride)
        outer_ref[place, :] = jnp.where(late, rows[1], rows[0])
        inner_ref[place, :] = jnp.where(late, rows[0], rows[1])

    for i in range(facet_rows):
        for j in range(facet_cols):
            rows = [
                rows_ref[pl.ds((2 * i + q) * facet_cols + j, chans, stride=per_chan), :] for q in range(2)
            ]
            store(i, j * block, chans, 1, rows)
    lane = lax.broadcasted_iota(jnp.int32, (per_chan, LANES), 1)
    column = lax.broadcasted_iota(jnp.int32, (per_chan, LANES), 0) % facet_cols
    for group in range(groups):
        left = jnp.zeros((per_chan, LANES), jnp.float32)
        right = jnp.zeros((per_chan, LANES), jnp.float32)
        on_left = lane < 0
        for slot in range(SLOTS):
            rows = rows_ref[pl.ds((group * SLOTS + slot) * per_chan, per_chan), :]
            start = 2 * HALO * slot
            here = (lane >= start) & (lane < start + HALO)
            on_left = on_left | here
            left = jnp.where(here, pltpu.roll(rows, (start + HALO) % LANES, 1), left)
            here = (lane >= start + HALO) & (lane < start + 2 * HALO)
            right = jnp.where(here, pltpu.roll(rows, start + HALO, 1), right)
        left = jnp.where(column > 0, pltpu.roll(left, 1, 0), 0.0)
        right = jnp.where(column < facet_cols - 1, pltpu.roll(right, per_chan - 1, 0), 0.0)
        sides = jnp.where(on_left, left, right)
        for i in range(facet_rows):
            first = 2 * i * facet_cols
            rows = [sides[first + q * facet_cols : first + (q + 1) * facet_cols] for q in range(2)]
            store(i, chans + group, facet_cols, block, rows)


def head_and_tail(values, lane, width):
    head, tail = split(values)
    middle = (lane >= width) & (lane < 2 * width)
    return jnp.where(middle, tail.astype(jnp.float32), head.astype(jnp.float32)).astype(jnp.bfloat16)


def prepare_kernel(me_ref, width_ref, outer_ref, inner_ref, centre_ref, sides_ref, vo_ref, vi_ref, w_ref, pad):
    odd = me_ref[1] % 2
    lane = lax.broadcasted_iota(jnp.int32, outer_ref.shape[1:], 1)
    place = lane % LANES
    first = jnp.where(odd == 1, HALF + EDGE - width_ref[0], EXT - width_ref[0])
    last = jnp.where(odd == 1, HALF + EDGE, HALF) + width_ref[0]
    above = (place >= first) & (place < first + width_ref[0])
    below = (place >= last - width_ref[0]) & (place < last)
    inside = (place < HALF) | above | below
    vo_ref[...] = head_and_tail(jnp.where(inside, outer_ref[odd], 0.0), lane, LANES)
    lane = lax.broadcasted_iota(jnp.int32, inner_ref.shape, 1)
    vi_ref[...] = head_and_tail(inner_ref[...], lane, HALF)
    place = lax.broadcasted_iota(jnp.int32, sides_ref.shape[1:], 0)
    before = jnp.where(place >= HALO - width_ref[1], sides_ref[0], 0.0)[:HALO]
    after = jnp.where(place < width_ref[1], sides_ref[1], 0.0)[:HALO]
    centre_head, centre_tail = split(centre_ref[...])
    for slot in range(SLOTS):
        pad[...] = jnp.zeros_like(pad)
        pad[2 * HALO * slot : 2 * HALO * slot + HALO, :] = before
        pad[2 * HALO * slot + HALO : 2 * HALO * (slot + 1), :] = after
        head, tail = split(pad[...])
        w_ref[slot] = jnp.concatenate(
            [centre_head, head, centre_head, head, centre_tail, tail], axis=0
        )


def outer_kernel(me_ref, in_ref, rows_ref, first_ref, second_ref, *, senders):
    odd = me_ref[1] % 2 == 1
    block = rows_ref.shape[0]
    for at in range(block):
        rows = in_ref[pl.ds(at, senders, stride=block), :]
        rows_ref[at] = rows
        top, bottom = rows[:EDGE], rows[CUT:]
        first_ref[at] = jnp.where(odd, top, bottom)
        second_ref[at] = jnp.where(odd, bottom, top)


def inner_kernel(in_ref, rows_ref, *, senders):
    block = rows_ref.shape[0]
    for at in range(block):
        rows_ref[at] = in_ref[pl.ds(at, senders, stride=block), :]


def project_kernel(rows_ref, nuc_ref, basis_ref, combined_ref, out_ref, *, chans, rank, outer):
    for start, size, is_outer, place in PIECES:
        if is_outer != outer:
            continue
        total = [None] * rank
        for ch in range(chans):
            block = nuc_ref[ch, pl.ds(start, size), :] + rows_ref[ch, pl.ds(place, size), :]
            combined_ref[ch, pl.ds(place, size), :] = block
            for k in range(rank):
                term = basis_ref[k, ch] * block
                total[k] = term if total[k] is None else total[k] + term
        for k in range(rank):
            out_ref[k, pl.ds(place, size), :] = total[k]


def filtered(ch, parts, sides, w_ref, v_ref, chans, gap):
    slot, group = ch % SLOTS, ch // SLOTS
    head, tail = split(jnp.concatenate([part[ch] for part in parts], axis=0))
    side_head, side_tail = sides[group]
    taken = jnp.concatenate([head, side_head, tail, side_tail, head, side_head], axis=1)
    across = jnp.dot(taken, w_ref[slot], preferred_element_type=jnp.float32)
    head, tail = split(across)
    stacked = [head, head, tail]
    if gap:
        nothing = jnp.zeros((gap, 2 * LANES), jnp.bfloat16)
        stacked = [head, nothing, head, nothing, tail, nothing]
    stacked = jnp.concatenate(stacked, axis=0)
    return jnp.dot(v_ref[...], stacked, preferred_element_type=jnp.float32)


def side_rows(parts, chans):
    return [
        split(jnp.concatenate([part[at] for part in parts], axis=0))
        for at in range(chans, parts[0].shape[0])
    ]


def order(chans):
    return [group * SLOTS + slot for slot in range(SLOTS) for group in range(chans // SLOTS)]


def quadrants(both):
    lane = lax.broadcasted_iota(jnp.int32, (HALF, LANES), 1)
    upper = jnp.where(lane < HALF, both[:HALF, :LANES], both[HALF:FACET, :LANES])
    return jnp.concatenate([upper, both[FACET:, LANES:]], axis=0)


def begin_kernel(rows_ref, first_ref, second_ref, v_ref, w_ref, wave_ref, out_ref, *, chans):
    parts = (rows_ref, first_ref, second_ref)
    sides = side_rows(parts, chans)
    for ch in order(chans):
        out_ref[ch] = wave_ref[ch] + quadrants(
            filtered(ch, parts, sides, w_ref, v_ref, chans, LANES - EXT)
        )


def wavelet_kernel(
    me_ref, band_ref, rows_ref, v_ref, w_ref, begun_ref, outer_ref, inner_ref,
    out_ref, own_ref, other_ref, squares, *, chans,
):
    core = me_ref[0] % 2
    chips = own_ref.shape[0]
    share = own_ref.shape[1] - FACET
    for chip in range(chips):
        for held, source in ((own_ref, 2 * chip + core), (other_ref, 2 * chip + 1 - core)):
            for start, size, is_outer, place in PIECES:
                part = outer_ref if is_outer else inner_ref
                held[chip, pl.ds(start, size), :] = part[source, pl.ds(place, size), :]
    squares[...] = jnp.zeros_like(squares)
    sides = side_rows((rows_ref,), chans)
    for ch in order(chans):
        dual = begun_ref[ch] + quadrants(filtered(ch, (rows_ref,), sides, w_ref, v_ref, chans, 0))
        out_ref[ch] = dual
        rows = pl.ds(pl.multiple_of(band_ref[ch] * FACET, FACET), FACET)
        squares[rows, :] = squares[rows, :] + dual * dual
    for chip in range(chips):
        first = pl.multiple_of((2 * chip + core) * share, share)
        own_ref[chip, FACET:, :] = squares[pl.ds(first, share), :]
        first = pl.multiple_of((2 * chip + 1 - core) * share, share)
        other_ref[chip, FACET:, :] = squares[pl.ds(first, share), :]


def pair_kernel(own_ref, came_ref, out_ref):
    out_ref[...] = own_ref[...] + came_ref[...]


def weigh_kernel(me_ref, thresh_ref, weight_ref, parts_ref, out_ref):
    chips = parts_ref.shape[0]
    total = parts_ref[0]
    for chip in range(1, chips):
        total = total + parts_ref[chip]
    spectrum, squares = total[:FACET], total[FACET:]
    threshold = thresh_ref[me_ref[0]]
    singular = jnp.sqrt(jnp.sum(spectrum * spectrum, keepdims=True))
    scaled = spectrum * (1.0 - threshold / jnp.maximum(singular, threshold))
    weight = weight_ref[me_ref[0]]
    ratio = weight / jnp.maximum(jnp.sqrt(squares), weight)
    for chip in range(chips):
        out_ref[chip, :FACET] = scaled
        out_ref[chip, FACET:] = ratio


def finish_kernel(
    me_ref, band_ref, basis_ref, outer_ref, inner_ref, dual_ref, own_ref, other_ref, wave_ref, nuc_ref,
    ordered, wave, nuc, sems, *, chans, rank,
):
    core, chips = me_ref[0] % 2, own_ref.shape[0]
    for chip in range(chips):
        ordered[2 * chip + core] = own_ref[chip]
        ordered[2 * chip + 1 - core] = other_ref[chip]
    share = ordered.shape[1] - FACET
    quarters = FACET // share
    copies = []
    for step, (start, size, is_outer, place) in enumerate(PIECES):
        rows = pl.ds(start, size)
        combined_ref = outer_ref if is_outer else inner_ref
        scaled = [ordered[k, rows, :] for k in range(rank)]
        for ch in range(chans):
            total = basis_ref[0, ch] * scaled[0]
            for k in range(1, rank):
                total = total + basis_ref[k, ch] * scaled[k]
            nuc[ch, rows, :] = combined_ref[ch, pl.ds(place, size), :] - total
            source = band_ref[ch] * quarters + start // share
            ratio = ordered[source, pl.ds(FACET + start % share, size), :]
            wave[ch, rows, :] = dual_ref[ch, rows, :] * ratio
        for kind, (held, out) in enumerate(((nuc, nuc_ref), (wave, wave_ref))):
            copy = pltpu.make_async_copy(held.at[:, rows, :], out.at[:, rows, :], sems.at[kind, step])
            copy.start()
            copies.append(copy)
    for copy in copies:
        copy.wait()


def call(kernel, name, ins, outs, operands, scratch=(), flops=0, limit=24, places=None):
    size = sum(4 * int(np.prod(o.shape)) for o in outs) + sum(4 * int(np.prod(o.shape)) for o in operands)
    return pl.pallas_call(
        kernel,
        name=name,
        in_specs=ins,
        out_specs=places or [VMEM] * len(outs),
        out_shape=outs,
        scratch_shapes=list(scratch),
        compiler_params=pltpu.CompilerParams(vmem_limit_bytes=limit * 1024 * 1024),
        cost_estimate=pl.CostEstimate(flops=flops, bytes_accessed=size, transcendentals=0),
    )(*operands)


def f32(*shape):
    return jax.ShapeDtypeStruct(shape, jnp.float32)


def bf16(*shape):
    return jax.ShapeDtypeStruct(shape, jnp.bfloat16)


def shards(primal_slab, wave_dual, nuc_dual, l21_weights, nuc_thresh, basis, band_of, margin_width):
    chans = wave_dual.shape[0]
    spec, rows, cols = (lax.axis_size(a) for a in ("spec", "frow", "fcol"))
    senders = rows * cols
    rank = basis.shape[3]
    bands = l21_weights.shape[0]
    plane = ("frow", "fcol")
    me = jnp.stack([lax.axis_index("spec"), lax.axis_index("frow")]).astype(jnp.int32)
    local_basis = basis.reshape(chans, rank).T
    bands_here = band_of.reshape(chans)
    widths = margin_width.reshape(2)

    block = chans + chans // SLOTS

    def redistribute(values):
        arrived = lax.all_to_all(
            values.reshape(senders, block, LANES), plane, split_axis=0, concat_axis=0, tiled=True
        )
        return arrived.reshape(-1, LANES)

    outer, inner = call(
        functools.partial(pack_kernel, chans=chans, facet_rows=rows, facet_cols=cols),
        "pack", [SMEM, VMEM], [f32(senders * block, LANES)] * 2,
        [me, primal_slab.reshape(-1, LANES)],
    )
    outer, inner = redistribute(outer), redistribute(inner)
    centre, sides = column_operators()
    outer_rows, inner_rows = row_operators()
    outer_filter, inner_filter, across = call(
        prepare_kernel, "prepare", [SMEM, SMEM] + [VMEM] * 4,
        [bf16(3 * HALF, 3 * LANES), bf16(3 * HALF, 3 * HALF), bf16(SLOTS, 6 * LANES, 2 * LANES)],
        [me, widths] + [jnp.asarray(m) for m in (outer_rows, inner_rows, centre, sides)],
        scratch=[pltpu.VMEM((LANES, 2 * LANES), jnp.float32)],
    )
    strip, halves = f32(block, EDGE, LANES), f32(block, HALF, LANES)
    outer, first, second = call(
        functools.partial(outer_kernel, senders=senders),
        "outer", [SMEM, VMEM], [halves, strip, strip], [me, outer],
    )
    first = lax.ppermute(first, "frow", [(i, i ^ 1) for i in range(rows)])
    other = [(i, i - 1 if i % 2 == 0 else i + 1) for i in range(1, rows - 1)]
    second = lax.ppermute(second, "frow", other)

    def project(values, is_outer):
        return call(
            functools.partial(project_kernel, chans=chans, rank=rank, outer=is_outer),
            "project", [VMEM, VMEM, SMEM],
            [f32(chans, HALF, LANES), f32(rank, HALF, LANES)],
            [values, nuc_dual, local_basis],
            flops=2 * chans * rank * HALF * LANES,
        )

    combined_outer, partial_outer = project(outer, True)
    (begun,) = call(
        functools.partial(begin_kernel, chans=chans),
        "begin", [VMEM] * 6, [f32(chans, FACET, LANES)],
        [outer, first, second, outer_filter, across, wave_dual],
        flops=2 * chans * 3 * 192 * 256 * 300,
    )
    (inner,) = call(functools.partial(inner_kernel, senders=senders), "inner", [VMEM], [halves], [inner])
    combined_inner, partial_inner = project(inner, False)
    share = bands * FACET // spec
    chips = spec // 2
    chunks = f32(chips, FACET + share, LANES)
    dual_sum, own, other = call(
        functools.partial(wavelet_kernel, chans=chans),
        "wavelet", [SMEM, SMEM] + [VMEM] * 6,
        [f32(chans, FACET, LANES), chunks, chunks],
        [me, bands_here, inner, inner_filter, across, begun, partial_outer, partial_inner],
        scratch=[pltpu.VMEM((bands * FACET, LANES), jnp.float32)],
        flops=2 * chans * 3 * 192 * 256 * 300,
    )

    def swap(values):
        return lax.ppermute(values, "spec", [(i, i ^ 1) for i in range(spec)])

    def across_chips(values):
        cores = [list(range(core, spec, 2)) for core in range(2)]
        return lax.all_to_all(
            values, "spec", split_axis=0, concat_axis=0, tiled=True, axis_index_groups=cores
        )

    (sums,) = call(pair_kernel, "pair", [VMEM, VMEM], [chunks], [own, swap(other)])
    (weighed,) = call(
        weigh_kernel, "weigh", [SMEM, SMEM, VMEM, VMEM], [chunks],
        [me, nuc_thresh.reshape(rank), l21_weights.reshape(spec, share, LANES), across_chips(sums)],
    )
    own = across_chips(weighed)
    wave_new, nuc_new = call(
        functools.partial(finish_kernel, chans=chans, rank=rank),
        "finish", [SMEM, SMEM, SMEM] + [VMEM] * 5,
        [f32(chans, FACET, LANES), f32(chans, FACET, LANES)],
        [me, bands_here, local_basis, combined_outer, combined_inner, dual_sum, own, swap(own)],
        scratch=[
            pltpu.VMEM((spec, FACET + share, LANES), jnp.float32),
            pltpu.VMEM((chans, FACET, LANES), jnp.float32),
            pltpu.VMEM((chans, FACET, LANES), jnp.float32),
            pltpu.SemaphoreType.DMA((2, len(PIECES))),
        ],
        flops=2 * chans * rank * FACET * LANES,
        places=[HBM, HBM],
    )
    return (wave_new, nuc_new)


def solution(mesh):
    return jax.shard_map(
        shards,
        mesh=mesh,
        in_specs=(
            P("spec", None, "frow", "fcol", None),
            P("spec", "frow", "fcol"),
            P("spec", "frow", "fcol"),
            P(None, "frow", "fcol"),
            P("frow", "fcol", None),
            P("frow", "fcol", "spec", None),
            P("frow", "fcol", "spec"),
            P("frow", "fcol", None),
        ),
        out_specs=(P("spec", "frow", "fcol"), P("spec", "frow", "fcol")),
        check_vma=False,
    )
```

```python
import functools

import jax
import jax.numpy as jnp
import numpy as np
from jax import lax
from jax.experimental import pallas as pl
from jax.experimental.pallas import tpu as pltpu
from jax.sharding import PartitionSpec as P

HALO = 21
EDGE = 24
SLOTS = 3
LANES = 128
FACET = 128
EXT = FACET + 2 * EDGE
VMEM = pl.BlockSpec(memory_space=pltpu.VMEM)
SMEM = pl.BlockSpec(memory_space=pltpu.SMEM)
HBM = pl.BlockSpec(memory_space=pltpu.HBM)

low_taps = [
    -0.00011747678400228192,
    0.0006754494059985568,
    -0.0003917403729959771,
    -0.00487035299301066,
    0.008746094047015655,
    0.013981027917015516,
    -0.04408825393106472,
    -0.01736930100202211,
    0.128747426620186,
    0.00047248457399797254,
    -0.2840155429624281,
    -0.015829105256023893,
    0.5853546836548691,
    0.6756307362980128,
    0.3128715909144659,
    0.05441584224308161,
]
tap_lag = 7
high_taps = [(-1.0) ** place * low_taps[15 - place] for place in range(16)]


def filter_matrix(in_length, taps, first, count):
    matrix = np.zeros((count, in_length))
    for out in range(count):
        matrix[out, 2 * (out + first) : 2 * (out + first) + 16] = taps
    return matrix


@functools.cache
def operators():
    length = FACET + 2 * HALO
    half, quarter = FACET // 2, FACET // 4
    low_all = filter_matrix(length, low_taps, 0, half + 14)
    high = filter_matrix(length, high_taps, tap_lag, half)
    low = low_all[tap_lag : tap_lag + half]
    coarse = np.concatenate(
        [
            filter_matrix(half + 14, low_taps, 0, quarter) @ low_all,
            filter_matrix(half + 14, high_taps, 0, quarter) @ low_all,
        ]
    )
    return coarse, low, high


def row_operator():
    whole = np.concatenate(operators())
    placed = np.zeros((2, whole.shape[0], 2 * LANES), np.float32)
    placed[:, :, :FACET] = whole[:, HALO : HALO + FACET]
    above, below = whole[:, :HALO], whole[:, HALO + FACET :]
    placed[0, :, FACET : FACET + HALO] = below
    placed[0, :, EXT - HALO : EXT] = above
    placed[1, :, FACET + EDGE - HALO : FACET + EDGE] = above
    placed[1, :, FACET + EDGE : FACET + EDGE + HALO] = below
    return placed


def column_operators():
    coarse, low, high = operators()
    whole = np.concatenate([coarse, high, low, high]).T.astype(np.float32)
    sides = np.zeros((2, EDGE, 2 * LANES), np.float32)
    sides[0, :HALO] = whole[:HALO]
    sides[1, :HALO] = whole[HALO + FACET :]
    return whole[HALO : HALO + FACET], sides


def split(values):
    head = values.astype(jnp.bfloat16)
    return head, (values - head.astype(jnp.float32)).astype(jnp.bfloat16)


def pack_kernel(me_ref, rows_ref, out_ref, *, chans, facet_rows, facet_cols, deal):
    block = deal * (chans + chans // SLOTS)
    per_chan = deal * facet_rows * facet_cols
    for i in range(facet_rows):
        for q in range(deal):
            for j in range(facet_cols):
                first = (deal * i + q) * facet_cols + j
                out_ref[pl.ds((i * facet_cols + j) * block + q * chans, chans), :] = rows_ref[
                    pl.ds(first, chans, stride=per_chan), :
                ]
    lane = lax.broadcasted_iota(jnp.int32, (per_chan, LANES), 1)
    column = lax.broadcasted_iota(jnp.int32, (per_chan, LANES), 0) % facet_cols
    for group in range(chans // SLOTS):
        left = jnp.zeros((per_chan, LANES), jnp.float32)
        right = jnp.zeros((per_chan, LANES), jnp.float32)
        on_left = lane < 0
        for slot in range(SLOTS):
            rows = rows_ref[pl.ds((group * SLOTS + slot) * per_chan, per_chan), :]
            start = 2 * HALO * slot
            here = (lane >= start) & (lane < start + HALO)
            on_left = on_left | here
            left = jnp.where(here, pltpu.roll(rows, (start + HALO) % LANES, 1), left)
            here = (lane >= start + HALO) & (lane < start + 2 * HALO)
            right = jnp.where(here, pltpu.roll(rows, start + HALO, 1), right)
        left = jnp.where(column > 0, pltpu.roll(left, 1, 0), 0.0)
        right = jnp.where(column < facet_cols - 1, pltpu.roll(right, per_chan - 1, 0), 0.0)
        sides = jnp.where(on_left, left, right)
        for i in range(facet_rows):
            for q in range(deal):
                first = (deal * i + q) * facet_cols
                place = i * facet_cols * block + deal * chans + q * (chans // SLOTS) + group
                out_ref[pl.ds(place, facet_cols, stride=block), :] = sides[first : first + facet_cols]


def prepare_kernel(me_ref, width_ref, rows_ref, centre_ref, sides_ref, v_ref, w_ref, pad):
    odd = 1 - me_ref[1] % 2
    lane = lax.broadcasted_iota(jnp.int32, rows_ref.shape[1:], 1)
    first = jnp.where(odd == 1, FACET + EDGE - width_ref[0], EXT - width_ref[0])
    last = jnp.where(odd == 1, FACET + EDGE, FACET) + width_ref[0]
    above = (lane >= first) & (lane < first + width_ref[0])
    below = (lane >= last - width_ref[0]) & (lane < last)
    head, tail = split(jnp.where((lane < FACET) | above | below, rows_ref[odd], 0.0))
    v_ref[:, : 2 * LANES] = head
    v_ref[:, 2 * LANES : 4 * LANES] = tail
    v_ref[:, 4 * LANES :] = head
    place = lax.broadcasted_iota(jnp.int32, sides_ref.shape[1:], 0)
    before = jnp.where(place >= HALO - width_ref[1], sides_ref[0], 0.0)[:HALO]
    after = jnp.where(place < width_ref[1], sides_ref[1], 0.0)[:HALO]
    centre_head, centre_tail = split(centre_ref[...])
    for slot in range(SLOTS):
        pad[...] = jnp.zeros_like(pad)
        pad[2 * HALO * slot : 2 * HALO * slot + HALO, :] = before
        pad[2 * HALO * slot + HALO : 2 * HALO * (slot + 1), :] = after
        head, tail = split(pad[...])
        w_ref[slot] = jnp.concatenate(
            [centre_head, head, centre_head, head, centre_tail, tail], axis=0
        )


def unpack_kernel(me_ref, in_ref, facet_ref, side_ref, first_ref, second_ref, *, chans, deal, senders):
    groups = chans // SLOTS
    block = deal * (chans + groups)
    odd = 1 - me_ref[1] % 2
    for at in range(chans + groups):
        if at < chans:
            starts = [q * chans + at for q in range(deal)]
        else:
            starts = [deal * chans + q * groups + at - chans for q in range(deal)]
        rows = jnp.concatenate([in_ref[pl.ds(s, senders, stride=block), :] for s in starts], axis=0)
        held, place = (facet_ref, at) if at < chans else (side_ref, at - chans)
        held[place] = rows
        top, bottom = rows[:EDGE], rows[FACET - EDGE :]
        first_ref[at] = jnp.where(odd == 1, top, bottom)
        second_ref[at] = jnp.where(odd == 1, bottom, top)


def project_kernel(facet_ref, nuc_ref, basis_ref, combined_ref, out_ref, *, chans, rank):
    for part in range(0, FACET, 32):
        rows = pl.ds(part, 32)
        total = [None] * rank
        for ch in range(chans):
            block = nuc_ref[ch, rows, :] + facet_ref[ch, rows, :]
            combined_ref[ch, rows, :] = block
            for k in range(rank):
                term = basis_ref[k, ch] * block
                total[k] = term if total[k] is None else total[k] + term
        for k in range(rank):
            out_ref[k, rows, :] = total[k]


def wavelet_kernel(
    me_ref, band_ref, facet_ref, side_ref, first_ref, second_ref, v_ref, w_ref, partial_ref, wave_ref,
    out_ref, own_ref, other_ref, squares, *, chans,
):
    core = me_ref[0] % 2
    chips = own_ref.shape[0]
    share = own_ref.shape[1] - FACET
    for chip in range(chips):
        own_ref[chip, :FACET, :] = partial_ref[2 * chip + core]
        other_ref[chip, :FACET, :] = partial_ref[2 * chip + 1 - core]
    squares[...] = jnp.zeros_like(squares)
    groups = chans // SLOTS
    half = FACET // 2
    lane = lax.broadcasted_iota(jnp.int32, (half, LANES), 1)
    nothing = jnp.zeros((2 * LANES - EXT, 2 * LANES), jnp.bfloat16)
    sides = [
        split(jnp.concatenate([side_ref[g], first_ref[chans + g], second_ref[chans + g]], axis=0))
        for g in range(groups)
    ]
    for slot in range(SLOTS):
        taken = []
        for group in range(groups):
            ch = group * SLOTS + slot
            head, tail = split(jnp.concatenate([facet_ref[ch], first_ref[ch], second_ref[ch]], axis=0))
            side_head, side_tail = sides[group]
            taken.append(jnp.concatenate([head, side_head, tail, side_tail, head, side_head], axis=1))
        across = jnp.dot(
            jnp.concatenate(taken, axis=0), w_ref[slot], preferred_element_type=jnp.float32
        )
        for group in range(groups):
            ch = group * SLOTS + slot
            head, tail = split(across[group * EXT : (group + 1) * EXT])
            stacked = jnp.concatenate([head, nothing, head, nothing, tail, nothing], axis=0)
            both = jnp.dot(v_ref[...], stacked, preferred_element_type=jnp.float32)
            upper = jnp.where(lane < half, both[:half, :LANES], both[half:FACET, :LANES])
            coeffs = jnp.concatenate([upper, both[FACET:, LANES:]], axis=0)
            dual = wave_ref[ch] + coeffs
            out_ref[ch] = dual
            rows = pl.ds(pl.multiple_of(band_ref[ch] * FACET, FACET), FACET)
            squares[rows, :] = squares[rows, :] + dual * dual
    for chip in range(chips):
        first = pl.multiple_of((2 * chip + core) * share, share)
        own_ref[chip, FACET:, :] = squares[pl.ds(first, share), :]
        first = pl.multiple_of((2 * chip + 1 - core) * share, share)
        other_ref[chip, FACET:, :] = squares[pl.ds(first, share), :]


def pair_kernel(own_ref, came_ref, out_ref):
    out_ref[...] = own_ref[...] + came_ref[...]


def weigh_kernel(me_ref, thresh_ref, weight_ref, parts_ref, out_ref):
    chips = parts_ref.shape[0]
    total = parts_ref[0]
    for chip in range(1, chips):
        total = total + parts_ref[chip]
    spectrum, squares = total[:FACET], total[FACET:]
    threshold = thresh_ref[me_ref[0]]
    singular = jnp.sqrt(jnp.sum(spectrum * spectrum, keepdims=True))
    scaled = spectrum * (1.0 - threshold / jnp.maximum(singular, threshold))
    weight = weight_ref[me_ref[0]]
    ratio = weight / jnp.maximum(jnp.sqrt(squares), weight)
    for chip in range(chips):
        out_ref[chip, :FACET] = scaled
        out_ref[chip, FACET:] = ratio


def finish_kernel(
    me_ref, band_ref, basis_ref, combined_ref, dual_ref, own_ref, other_ref, wave_ref, nuc_ref,
    ordered, wave, nuc, sems, *, chans, rank,
):
    core, chips = me_ref[0] % 2, own_ref.shape[0]
    for chip in range(chips):
        ordered[2 * chip + core] = own_ref[chip]
        ordered[2 * chip + 1 - core] = other_ref[chip]
    share = ordered.shape[1] - FACET
    pieces = FACET // share
    copies = []
    for part in range(pieces):
        rows = pl.ds(part * share, share)
        scaled = [ordered[k, rows, :] for k in range(rank)]
        for ch in range(chans):
            total = basis_ref[0, ch] * scaled[0]
            for k in range(1, rank):
                total = total + basis_ref[k, ch] * scaled[k]
            nuc[ch, rows, :] = combined_ref[ch, rows, :] - total
            ratio = ordered[band_ref[ch] * pieces + part, FACET:, :]
            wave[ch, rows, :] = dual_ref[ch, rows, :] * ratio
        for place, (held, out) in enumerate(((nuc, nuc_ref), (wave, wave_ref))):
            copy = pltpu.make_async_copy(held.at[:, rows, :], out.at[:, rows, :], sems.at[place, part])
            copy.start()
            copies.append(copy)
    for copy in copies:
        copy.wait()


def call(kernel, name, ins, outs, operands, scratch=(), flops=0, limit=24, places=None):
    size = sum(4 * int(np.prod(o.shape)) for o in outs) + sum(4 * int(np.prod(o.shape)) for o in operands)
    return pl.pallas_call(
        kernel,
        name=name,
        in_specs=ins,
        out_specs=places or [VMEM] * len(outs),
        out_shape=outs,
        scratch_shapes=list(scratch),
        compiler_params=pltpu.CompilerParams(vmem_limit_bytes=limit * 1024 * 1024),
        cost_estimate=pl.CostEstimate(flops=flops, bytes_accessed=size, transcendentals=0),
    )(*operands)


def f32(*shape):
    return jax.ShapeDtypeStruct(shape, jnp.float32)


def bf16(*shape):
    return jax.ShapeDtypeStruct(shape, jnp.bfloat16)


def shards(primal_slab, wave_dual, nuc_dual, l21_weights, nuc_thresh, basis, band_of, margin_width):
    chans = wave_dual.shape[0]
    spec, rows, cols = (lax.axis_size(a) for a in ("spec", "frow", "fcol"))
    senders = rows * cols
    deal = primal_slab.shape[1] // rows
    rank = basis.shape[3]
    bands = l21_weights.shape[0]
    plane = ("frow", "fcol")
    me = jnp.stack([lax.axis_index("spec"), lax.axis_index("frow")]).astype(jnp.int32)
    local_basis = basis.reshape(chans, rank).T
    bands_here = band_of.reshape(chans)
    widths = margin_width.reshape(2)

    groups = chans // SLOTS
    block = deal * (chans + groups)
    (packed,) = call(
        functools.partial(pack_kernel, chans=chans, facet_rows=rows, facet_cols=cols, deal=deal),
        "pack", [SMEM, VMEM], [f32(senders * block, LANES)],
        [me, primal_slab.reshape(-1, LANES)],
    )
    arrived = lax.all_to_all(
        packed.reshape(senders, block, LANES), plane, split_axis=0, concat_axis=0, tiled=True
    )
    centre, sides = column_operators()
    vertical, across = call(
        prepare_kernel, "prepare", [SMEM, SMEM, VMEM, VMEM, VMEM],
        [bf16(3 * FACET // 2, 6 * LANES), bf16(SLOTS, 6 * LANES, 2 * LANES)],
        [me, widths, jnp.asarray(row_operator()), jnp.asarray(centre), jnp.asarray(sides)],
        scratch=[pltpu.VMEM((LANES, 2 * LANES), jnp.float32)],
    )
    strip = f32(chans + groups, EDGE, LANES)
    facet, side, first, second = call(
        functools.partial(unpack_kernel, chans=chans, deal=deal, senders=senders),
        "unpack", [SMEM, VMEM],
        [f32(chans, FACET, LANES), f32(groups, FACET, LANES), strip, strip],
        [me, arrived.reshape(-1, LANES)],
    )
    inward = [(i, i - 1 if i % 2 == 0 else i + 1) for i in range(1, rows - 1)]
    first = lax.ppermute(first, "frow", inward)
    second = lax.ppermute(second, "frow", [(i, i ^ 1) for i in range(rows)])
    combined, partial = call(
        functools.partial(project_kernel, chans=chans, rank=rank),
        "project", [VMEM, VMEM, SMEM],
        [f32(chans, FACET, LANES), f32(rank, FACET, LANES)],
        [facet, nuc_dual, local_basis],
        flops=2 * chans * rank * FACET * LANES,
    )
    share = bands * FACET // spec
    chips = spec // 2
    chunks = f32(chips, FACET + share, LANES)
    dual_sum, own, other = call(
        functools.partial(wavelet_kernel, chans=chans),
        "wavelet", [SMEM, SMEM] + [VMEM] * 8,
        [f32(chans, FACET, LANES), chunks, chunks],
        [me, bands_here, facet, side, first, second, vertical, across, partial, wave_dual],
        scratch=[
            pltpu.VMEM((bands * FACET, LANES), jnp.float32),
        ],
        flops=2 * chans * 3 * 192 * 256 * 600,
    )

    def swap(values):
        return lax.ppermute(values, "spec", [(i, i ^ 1) for i in range(spec)])

    def across_chips(values):
        cores = [list(range(core, spec, 2)) for core in range(2)]
        return lax.all_to_all(
            values, "spec", split_axis=0, concat_axis=0, tiled=True, axis_index_groups=cores
        )

    (sums,) = call(pair_kernel, "pair", [VMEM, VMEM], [chunks], [own, swap(other)])
    (weighed,) = call(
        weigh_kernel, "weigh", [SMEM, SMEM, VMEM, VMEM], [chunks],
        [me, nuc_thresh.reshape(rank), l21_weights.reshape(spec, share, LANES), across_chips(sums)],
    )
    own = across_chips(weighed)
    wave_new, nuc_new = call(
        functools.partial(finish_kernel, chans=chans, rank=rank),
        "finish", [SMEM, SMEM, SMEM] + [VMEM] * 4,
        [f32(chans, FACET, LANES), f32(chans, FACET, LANES)],
        [me, bands_here, local_basis, combined, dual_sum, own, swap(own)],
        scratch=[
            pltpu.VMEM((spec, FACET + share, LANES), jnp.float32),
            pltpu.VMEM((chans, FACET, LANES), jnp.float32),
            pltpu.VMEM((chans, FACET, LANES), jnp.float32),
            pltpu.SemaphoreType.DMA((2, FACET // share)),
        ],
        flops=2 * chans * rank * FACET * LANES,
        places=[HBM, HBM],
    )
    return (wave_new, nuc_new)


def solution(mesh):
    return jax.shard_map(
        shards,
        mesh=mesh,
        in_specs=(
            P("spec", None, "frow", "fcol", None),
            P("spec", "frow", "fcol"),
            P("spec", "frow", "fcol"),
            P(None, "frow", "fcol"),
            P("frow", "fcol", None),
            P("frow", "fcol", "spec", None),
            P("frow", "fcol", "spec"),
            P("frow", "fcol", None),
        ),
        out_specs=(P("spec", "frow", "fcol"), P("spec", "frow", "fcol")),
        check_vma=False,
    )
```

```python
import functools

import jax
import jax.numpy as jnp
import numpy as np
from jax import lax
from jax.experimental import pallas as pl
from jax.experimental.pallas import tpu as pltpu
from jax.sharding import PartitionSpec as P

HALO = 21
EDGE = 24
SLOTS = 3
LANES = 128
FACET = 128
EXT = FACET + 2 * EDGE
VMEM = pl.BlockSpec(memory_space=pltpu.VMEM)
SMEM = pl.BlockSpec(memory_space=pltpu.SMEM)
HBM = pl.BlockSpec(memory_space=pltpu.HBM)

low_taps = [
    -0.00011747678400228192,
    0.0006754494059985568,
    -0.0003917403729959771,
    -0.00487035299301066,
    0.008746094047015655,
    0.013981027917015516,
    -0.04408825393106472,
    -0.01736930100202211,
    0.128747426620186,
    0.00047248457399797254,
    -0.2840155429624281,
    -0.015829105256023893,
    0.5853546836548691,
    0.6756307362980128,
    0.3128715909144659,
    0.05441584224308161,
]
tap_lag = 7
high_taps = [(-1.0) ** place * low_taps[15 - place] for place in range(16)]


def filter_matrix(in_length, taps, first, count):
    matrix = np.zeros((count, in_length))
    for out in range(count):
        matrix[out, 2 * (out + first) : 2 * (out + first) + 16] = taps
    return matrix


@functools.cache
def operators():
    length = FACET + 2 * HALO
    half, quarter = FACET // 2, FACET // 4
    low_all = filter_matrix(length, low_taps, 0, half + 14)
    high = filter_matrix(length, high_taps, tap_lag, half)
    low = low_all[tap_lag : tap_lag + half]
    coarse = np.concatenate(
        [
            filter_matrix(half + 14, low_taps, 0, quarter) @ low_all,
            filter_matrix(half + 14, high_taps, 0, quarter) @ low_all,
        ]
    )
    return coarse, low, high


def row_operator():
    whole = np.concatenate(operators())
    placed = np.zeros((2, whole.shape[0], 2 * LANES), np.float32)
    placed[:, :, :FACET] = whole[:, HALO : HALO + FACET]
    above, below = whole[:, :HALO], whole[:, HALO + FACET :]
    placed[0, :, FACET : FACET + HALO] = below
    placed[0, :, EXT - HALO : EXT] = above
    placed[1, :, FACET + EDGE - HALO : FACET + EDGE] = above
    placed[1, :, FACET + EDGE : FACET + EDGE + HALO] = below
    return placed


def column_operators():
    coarse, low, high = operators()
    whole = np.concatenate([coarse, high, low, high]).T.astype(np.float32)
    sides = np.zeros((2, EDGE, 2 * LANES), np.float32)
    sides[0, :HALO] = whole[:HALO]
    sides[1, :HALO] = whole[HALO + FACET :]
    return whole[HALO : HALO + FACET], sides


def split(values):
    head = values.astype(jnp.bfloat16)
    return head, (values - head.astype(jnp.float32)).astype(jnp.bfloat16)


def pack_kernel(me_ref, rows_ref, out_ref, *, chans, facet_rows, facet_cols, deal):
    block = deal * (chans + chans // SLOTS)
    per_chan = deal * facet_rows * facet_cols
    for i in range(facet_rows):
        for q in range(deal):
            for j in range(facet_cols):
                first = (deal * i + q) * facet_cols + j
                out_ref[pl.ds((i * facet_cols + j) * block + q * chans, chans), :] = rows_ref[
                    pl.ds(first, chans, stride=per_chan), :
                ]
    lane = lax.broadcasted_iota(jnp.int32, (per_chan, LANES), 1)
    column = lax.broadcasted_iota(jnp.int32, (per_chan, LANES), 0) % facet_cols
    for group in range(chans // SLOTS):
        left = jnp.zeros((per_chan, LANES), jnp.float32)
        right = jnp.zeros((per_chan, LANES), jnp.float32)
        on_left = lane < 0
        for slot in range(SLOTS):
            rows = rows_ref[pl.ds((group * SLOTS + slot) * per_chan, per_chan), :]
            start = 2 * HALO * slot
            here = (lane >= start) & (lane < start + HALO)
            on_left = on_left | here
            left = jnp.where(here, pltpu.roll(rows, (start + HALO) % LANES, 1), left)
            here = (lane >= start + HALO) & (lane < start + 2 * HALO)
            right = jnp.where(here, pltpu.roll(rows, start + HALO, 1), right)
        left = jnp.where(column > 0, pltpu.roll(left, 1, 0), 0.0)
        right = jnp.where(column < facet_cols - 1, pltpu.roll(right, per_chan - 1, 0), 0.0)
        sides = jnp.where(on_left, left, right)
        for i in range(facet_rows):
            for q in range(deal):
                first = (deal * i + q) * facet_cols
                place = i * facet_cols * block + deal * chans + q * (chans // SLOTS) + group
                out_ref[pl.ds(place, facet_cols, stride=block), :] = sides[first : first + facet_cols]


def prepare_kernel(me_ref, width_ref, rows_ref, centre_ref, sides_ref, v_ref, w_ref, pad):
    odd = 1 - me_ref[1] % 2
    lane = lax.broadcasted_iota(jnp.int32, rows_ref.shape[1:], 1)
    first = jnp.where(odd == 1, FACET + EDGE - width_ref[0], EXT - width_ref[0])
    last = jnp.where(odd == 1, FACET + EDGE, FACET) + width_ref[0]
    above = (lane >= first) & (lane < first + width_ref[0])
    below = (lane >= last - width_ref[0]) & (lane < last)
    head, tail = split(jnp.where((lane < FACET) | above | below, rows_ref[odd], 0.0))
    v_ref[:, : 2 * LANES] = head
    v_ref[:, 2 * LANES : 4 * LANES] = tail
    v_ref[:, 4 * LANES :] = head
    place = lax.broadcasted_iota(jnp.int32, sides_ref.shape[1:], 0)
    before = jnp.where(place >= HALO - width_ref[1], sides_ref[0], 0.0)[:HALO]
    after = jnp.where(place < width_ref[1], sides_ref[1], 0.0)[:HALO]
    centre_head, centre_tail = split(centre_ref[...])
    for slot in range(SLOTS):
        pad[...] = jnp.zeros_like(pad)
        pad[2 * HALO * slot : 2 * HALO * slot + HALO, :] = before
        pad[2 * HALO * slot + HALO : 2 * HALO * (slot + 1), :] = after
        head, tail = split(pad[...])
        w_ref[slot] = jnp.concatenate(
            [centre_head, head, centre_head, head, centre_tail, tail], axis=0
        )


def unpack_kernel(me_ref, in_ref, facet_ref, side_ref, first_ref, second_ref, *, chans, deal, senders):
    groups = chans // SLOTS
    block = deal * (chans + groups)
    odd = 1 - me_ref[1] % 2
    for at in range(chans + groups):
        if at < chans:
            starts = [q * chans + at for q in range(deal)]
        else:
            starts = [deal * chans + q * groups + at - chans for q in range(deal)]
        rows = jnp.concatenate([in_ref[pl.ds(s, senders, stride=block), :] for s in starts], axis=0)
        held, place = (facet_ref, at) if at < chans else (side_ref, at - chans)
        held[place] = rows
        top, bottom = rows[:EDGE], rows[FACET - EDGE :]
        first_ref[at] = jnp.where(odd == 1, top, bottom)
        second_ref[at] = jnp.where(odd == 1, bottom, top)


def project_kernel(
    me_ref, facet_ref, nuc_ref, basis_ref, combined_ref, own_ref, other_ref, *, chans, rank
):
    even = me_ref[0] % 2 == 0
    for part in range(0, FACET, 32):
        rows = pl.ds(part, 32)
        total = [None] * rank
        for ch in range(chans):
            block = nuc_ref[ch, rows, :] + facet_ref[ch, rows, :]
            combined_ref[ch, rows, :] = block
            for k in range(rank):
                term = basis_ref[k, ch] * block
                total[k] = term if total[k] is None else total[k] + term
        for chip in range(rank // 2):
            first, second = total[2 * chip], total[2 * chip + 1]
            own_ref[chip, rows, :] = jnp.where(even, first, second)
            other_ref[chip, rows, :] = jnp.where(even, second, first)


def wavelet_kernel(
    me_ref, band_ref, facet_ref, side_ref, first_ref, second_ref, v_ref, w_ref, wave_ref,
    out_ref, own_ref, other_ref, squares, *, chans,
):
    squares[...] = jnp.zeros_like(squares)
    groups = chans // SLOTS
    half = FACET // 2
    lane = lax.broadcasted_iota(jnp.int32, (half, LANES), 1)
    nothing = jnp.zeros((2 * LANES - EXT, 2 * LANES), jnp.bfloat16)
    sides = [
        split(jnp.concatenate([side_ref[g], first_ref[chans + g], second_ref[chans + g]], axis=0))
        for g in range(groups)
    ]
    for slot in range(SLOTS):
        taken = []
        for group in range(groups):
            ch = group * SLOTS + slot
            head, tail = split(jnp.concatenate([facet_ref[ch], first_ref[ch], second_ref[ch]], axis=0))
            side_head, side_tail = sides[group]
            taken.append(jnp.concatenate([head, side_head, tail, side_tail, head, side_head], axis=1))
        across = jnp.dot(
            jnp.concatenate(taken, axis=0), w_ref[slot], preferred_element_type=jnp.float32
        )
        for group in range(groups):
            ch = group * SLOTS + slot
            head, tail = split(across[group * EXT : (group + 1) * EXT])
            stacked = jnp.concatenate([head, nothing, head, nothing, tail, nothing], axis=0)
            both = jnp.dot(v_ref[...], stacked, preferred_element_type=jnp.float32)
            upper = jnp.where(lane < half, both[:half, :LANES], both[half:FACET, :LANES])
            coeffs = jnp.concatenate([upper, both[FACET:, LANES:]], axis=0)
            dual = wave_ref[ch] + coeffs
            out_ref[ch] = dual
            rows = pl.ds(pl.multiple_of(band_ref[ch] * FACET, FACET), FACET)
            squares[rows, :] = squares[rows, :] + dual * dual
    core = me_ref[0] % 2
    own_ref[...] = squares[pl.ds(pl.multiple_of(core * FACET, FACET), FACET), :]
    other_ref[...] = squares[pl.ds(pl.multiple_of((1 - core) * FACET, FACET), FACET), :]


def pair_kernel(own_ref, came_ref, out_ref):
    out_ref[...] = own_ref[...] + came_ref[...]


def weigh_kernel(me_ref, thresh_ref, parts_ref, own_ref, came_ref, out_ref):
    chips = parts_ref.shape[0]
    spectrum = parts_ref[0]
    for chip in range(1, chips):
        spectrum = spectrum + parts_ref[chip]
    threshold = thresh_ref[me_ref[0]]
    singular = jnp.sqrt(jnp.sum(spectrum * spectrum, keepdims=True))
    scaled = spectrum * (1.0 - threshold / jnp.maximum(singular, threshold))
    squares = own_ref[...] + came_ref[...]
    for chip in range(chips):
        out_ref[chip, :FACET] = scaled
        out_ref[chip, FACET:] = squares


def ratio_kernel(me_ref, weight_ref, parts_ref, out_ref):
    chips = parts_ref.shape[0]
    squares = parts_ref[0, FACET:]
    for chip in range(1, chips):
        squares = squares + parts_ref[chip, FACET:]
    weight = weight_ref[me_ref[0] % 2]
    for chip in range(chips):
        out_ref[chip] = parts_ref[chip, :FACET]
    out_ref[chips] = weight / jnp.maximum(jnp.sqrt(squares), weight)


def finish_kernel(
    me_ref, band_ref, basis_ref, combined_ref, dual_ref, own_ref, other_ref, wave_ref, nuc_ref,
    ordered, wave, nuc, sems, *, chans, rank,
):
    core, places = me_ref[0] % 2, own_ref.shape[0]
    for place in range(places):
        ordered[2 * place + core] = own_ref[place]
        ordered[2 * place + 1 - core] = other_ref[place]
    copies = []
    for step, start in enumerate(range(0, FACET, 32)):
        rows = pl.ds(start, 32)
        scaled = [ordered[k, rows, :] for k in range(rank)]
        for ch in range(chans):
            total = basis_ref[0, ch] * scaled[0]
            for k in range(1, rank):
                total = total + basis_ref[k, ch] * scaled[k]
            nuc[ch, rows, :] = combined_ref[ch, rows, :] - total
            wave[ch, rows, :] = dual_ref[ch, rows, :] * ordered[rank + band_ref[ch], rows, :]
        for kind, (held, out) in enumerate(((nuc, nuc_ref), (wave, wave_ref))):
            copy = pltpu.make_async_copy(held.at[:, rows, :], out.at[:, rows, :], sems.at[kind, step])
            copy.start()
            copies.append(copy)
    for copy in copies:
        copy.wait()


def call(kernel, name, ins, outs, operands, scratch=(), flops=0, limit=24, places=None):
    size = sum(4 * int(np.prod(o.shape)) for o in outs) + sum(4 * int(np.prod(o.shape)) for o in operands)
    return pl.pallas_call(
        kernel,
        name=name,
        in_specs=ins,
        out_specs=places or [VMEM] * len(outs),
        out_shape=outs,
        scratch_shapes=list(scratch),
        compiler_params=pltpu.CompilerParams(vmem_limit_bytes=limit * 1024 * 1024),
        cost_estimate=pl.CostEstimate(flops=flops, bytes_accessed=size, transcendentals=0),
    )(*operands)


def f32(*shape):
    return jax.ShapeDtypeStruct(shape, jnp.float32)


def bf16(*shape):
    return jax.ShapeDtypeStruct(shape, jnp.bfloat16)


def shards(primal_slab, wave_dual, nuc_dual, l21_weights, nuc_thresh, basis, band_of, margin_width):
    chans = wave_dual.shape[0]
    spec, rows, cols = (lax.axis_size(a) for a in ("spec", "frow", "fcol"))
    senders = rows * cols
    deal = primal_slab.shape[1] // rows
    rank = basis.shape[3]
    bands = l21_weights.shape[0]
    plane = ("frow", "fcol")
    me = jnp.stack([lax.axis_index("spec"), lax.axis_index("frow")]).astype(jnp.int32)
    local_basis = basis.reshape(chans, rank).T
    bands_here = band_of.reshape(chans)
    widths = margin_width.reshape(2)

    groups = chans // SLOTS
    block = deal * (chans + groups)
    (packed,) = call(
        functools.partial(pack_kernel, chans=chans, facet_rows=rows, facet_cols=cols, deal=deal),
        "pack", [SMEM, VMEM], [f32(senders * block, LANES)],
        [me, primal_slab.reshape(-1, LANES)],
    )
    arrived = lax.all_to_all(
        packed.reshape(senders, block, LANES), plane, split_axis=0, concat_axis=0, tiled=True
    )
    centre, sides = column_operators()
    vertical, across = call(
        prepare_kernel, "prepare", [SMEM, SMEM, VMEM, VMEM, VMEM],
        [bf16(3 * FACET // 2, 6 * LANES), bf16(SLOTS, 6 * LANES, 2 * LANES)],
        [me, widths, jnp.asarray(row_operator()), jnp.asarray(centre), jnp.asarray(sides)],
        scratch=[pltpu.VMEM((LANES, 2 * LANES), jnp.float32)],
    )
    strip = f32(chans + groups, EDGE, LANES)
    facet, side, first, second = call(
        functools.partial(unpack_kernel, chans=chans, deal=deal, senders=senders),
        "unpack", [SMEM, VMEM],
        [f32(chans, FACET, LANES), f32(groups, FACET, LANES), strip, strip],
        [me, arrived.reshape(-1, LANES)],
    )
    inward = [(i, i - 1 if i % 2 == 0 else i + 1) for i in range(1, rows - 1)]
    first = lax.ppermute(first, "frow", inward)
    second = lax.ppermute(second, "frow", [(i, i ^ 1) for i in range(rows)])
    chips = spec // 2
    plane_sums, ranks = f32(FACET, LANES), f32(chips, FACET, LANES)

    def swap(values):
        return lax.ppermute(values, "spec", [(i, i ^ 1) for i in range(spec)])

    def across_chips(values):
        cores = [list(range(core, spec, 2)) for core in range(2)]
        return lax.all_to_all(
            values, "spec", split_axis=0, concat_axis=0, tiled=True, axis_index_groups=cores
        )

    combined, own, other = call(
        functools.partial(project_kernel, chans=chans, rank=rank),
        "project", [SMEM, VMEM, VMEM, SMEM],
        [f32(chans, FACET, LANES), ranks, ranks],
        [me, facet, nuc_dual, local_basis],
        flops=2 * chans * rank * FACET * LANES,
    )
    (sums,) = call(pair_kernel, "pair", [VMEM, VMEM], [ranks], [own, swap(other)])
    parts = across_chips(sums)
    dual_sum, own, other = call(
        functools.partial(wavelet_kernel, chans=chans),
        "wavelet", [SMEM, SMEM] + [VMEM] * 7,
        [f32(chans, FACET, LANES), plane_sums, plane_sums],
        [me, bands_here, facet, side, first, second, vertical, across, wave_dual],
        scratch=[pltpu.VMEM((bands * FACET, LANES), jnp.float32)],
        flops=2 * chans * 3 * 192 * 256 * 600,
    )
    (weighed,) = call(
        weigh_kernel, "weigh", [SMEM, SMEM, VMEM, VMEM, VMEM], [f32(chips, 2 * FACET, LANES)],
        [me, nuc_thresh.reshape(rank), parts, own, swap(other)],
    )
    (own,) = call(
        ratio_kernel, "ratio", [SMEM, VMEM, VMEM], [f32(chips + 1, FACET, LANES)],
        [me, l21_weights, across_chips(weighed)],
    )
    wave_new, nuc_new = call(
        functools.partial(finish_kernel, chans=chans, rank=rank),
        "finish", [SMEM, SMEM, SMEM] + [VMEM] * 4,
        [f32(chans, FACET, LANES), f32(chans, FACET, LANES)],
        [me, bands_here, local_basis, combined, dual_sum, own, swap(own)],
        scratch=[
            pltpu.VMEM((rank + bands, FACET, LANES), jnp.float32),
            pltpu.VMEM((chans, FACET, LANES), jnp.float32),
            pltpu.VMEM((chans, FACET, LANES), jnp.float32),
            pltpu.SemaphoreType.DMA((2, FACET // 32)),
        ],
        flops=2 * chans * rank * FACET * LANES,
        places=[HBM, HBM],
    )
    return (wave_new, nuc_new)


def solution(mesh):
    return jax.shard_map(
        shards,
        mesh=mesh,
        in_specs=(
            P("spec", None, "frow", "fcol", None),
            P("spec", "frow", "fcol"),
            P("spec", "frow", "fcol"),
            P(None, "frow", "fcol"),
            P("frow", "fcol", None),
            P("frow", "fcol", "spec", None),
            P("frow", "fcol", "spec"),
            P("frow", "fcol", None),
        ),
        out_specs=(P("spec", "frow", "fcol"), P("spec", "frow", "fcol")),
        check_vma=False,
    )
```

```python
import functools

import jax
import jax.numpy as jnp
import numpy as np
from jax import lax
from jax.experimental import pallas as pl
from jax.experimental.pallas import tpu as pltpu
from jax.sharding import PartitionSpec as P

HALO = 21
EDGE = 24
SLOTS = 3
LANES = 128
FACET = 128
EXT = FACET + 2 * EDGE
VMEM = pl.BlockSpec(memory_space=pltpu.VMEM)
SMEM = pl.BlockSpec(memory_space=pltpu.SMEM)
HBM = pl.BlockSpec(memory_space=pltpu.HBM)

low_taps = [
    -0.00011747678400228192,
    0.0006754494059985568,
    -0.0003917403729959771,
    -0.00487035299301066,
    0.008746094047015655,
    0.013981027917015516,
    -0.04408825393106472,
    -0.01736930100202211,
    0.128747426620186,
    0.00047248457399797254,
    -0.2840155429624281,
    -0.015829105256023893,
    0.5853546836548691,
    0.6756307362980128,
    0.3128715909144659,
    0.05441584224308161,
]
tap_lag = 7
high_taps = [(-1.0) ** place * low_taps[15 - place] for place in range(16)]


def filter_matrix(in_length, taps, first, count):
    matrix = np.zeros((count, in_length))
    for out in range(count):
        matrix[out, 2 * (out + first) : 2 * (out + first) + 16] = taps
    return matrix


@functools.cache
def operators():
    length = FACET + 2 * HALO
    half, quarter = FACET // 2, FACET // 4
    low_all = filter_matrix(length, low_taps, 0, half + 14)
    high = filter_matrix(length, high_taps, tap_lag, half)
    low = low_all[tap_lag : tap_lag + half]
    coarse = np.concatenate(
        [
            filter_matrix(half + 14, low_taps, 0, quarter) @ low_all,
            filter_matrix(half + 14, high_taps, 0, quarter) @ low_all,
        ]
    )
    return coarse, low, high


def row_operator():
    whole = np.concatenate(operators())
    placed = np.zeros((2, whole.shape[0], 2 * LANES), np.float32)
    placed[:, :, :FACET] = whole[:, HALO : HALO + FACET]
    above, below = whole[:, :HALO], whole[:, HALO + FACET :]
    placed[0, :, FACET : FACET + HALO] = below
    placed[0, :, EXT - HALO : EXT] = above
    placed[1, :, FACET + EDGE - HALO : FACET + EDGE] = above
    placed[1, :, FACET + EDGE : FACET + EDGE + HALO] = below
    return placed


def column_operators():
    coarse, low, high = operators()
    whole = np.concatenate([coarse, high, low, high]).T.astype(np.float32)
    sides = np.zeros((2, EDGE, 2 * LANES), np.float32)
    sides[0, :HALO] = whole[:HALO]
    sides[1, :HALO] = whole[HALO + FACET :]
    return whole[HALO : HALO + FACET], sides


def spec_index():
    return lax.axis_index("spec").astype(jnp.int32)


def even_row():
    return lax.rem(lax.axis_index("frow").astype(jnp.int32), 2) == 0


def split(values):
    head = values.astype(jnp.bfloat16)
    return head, (values - head.astype(jnp.float32)).astype(jnp.bfloat16)


def pack_kernel(rows_ref, out_ref, *, chans, facet_rows, facet_cols, deal):
    block = deal * (chans + chans // SLOTS)
    per_chan = deal * facet_rows * facet_cols
    for i in range(facet_rows):
        for q in range(deal):
            for j in range(facet_cols):
                first = (deal * i + q) * facet_cols + j
                out_ref[pl.ds((i * facet_cols + j) * block + q * chans, chans), :] = rows_ref[
                    pl.ds(first, chans, stride=per_chan), :
                ]
    lane = lax.broadcasted_iota(jnp.int32, (per_chan, LANES), 1)
    column = lax.broadcasted_iota(jnp.int32, (per_chan, LANES), 0) % facet_cols
    for group in range(chans // SLOTS):
        left = jnp.zeros((per_chan, LANES), jnp.float32)
        right = jnp.zeros((per_chan, LANES), jnp.float32)
        on_left = lane < 0
        for slot in range(SLOTS):
            rows = rows_ref[pl.ds((group * SLOTS + slot) * per_chan, per_chan), :]
            start = 2 * HALO * slot
            here = (lane >= start) & (lane < start + HALO)
            on_left = on_left | here
            left = jnp.where(here, pltpu.roll(rows, (start + HALO) % LANES, 1), left)
            here = (lane >= start + HALO) & (lane < start + 2 * HALO)
            right = jnp.where(here, pltpu.roll(rows, start + HALO, 1), right)
        left = jnp.where(column > 0, pltpu.roll(left, 1, 0), 0.0)
        right = jnp.where(column < facet_cols - 1, pltpu.roll(right, per_chan - 1, 0), 0.0)
        sides = jnp.where(on_left, left, right)
        for i in range(facet_rows):
            for q in range(deal):
                first = (deal * i + q) * facet_cols
                place = i * facet_cols * block + deal * chans + q * (chans // SLOTS) + group
                out_ref[pl.ds(place, facet_cols, stride=block), :] = sides[first : first + facet_cols]


def prepare_kernel(
    width_ref, basis_ref, band_ref, rows_ref, centre_ref, sides_ref,
    v_ref, w_ref, spread_ref, pick_ref, pad,
):
    rank, chans = basis_ref.shape
    for ch in range(chans):
        pick_ref[ch] = jnp.full((8, LANES), band_ref[ch], jnp.int32)
        for k in range(rank):
            spread_ref[k, ch] = jnp.full((8, LANES), basis_ref[k, ch], jnp.float32)
    odd = even_row().astype(jnp.int32)
    lane = lax.broadcasted_iota(jnp.int32, rows_ref.shape[1:], 1)
    first = jnp.where(odd == 1, FACET + EDGE - width_ref[0], EXT - width_ref[0])
    last = jnp.where(odd == 1, FACET + EDGE, FACET) + width_ref[0]
    above = (lane >= first) & (lane < first + width_ref[0])
    below = (lane >= last - width_ref[0]) & (lane < last)
    head, tail = split(jnp.where((lane < FACET) | above | below, rows_ref[odd], 0.0))
    v_ref[:, : 2 * LANES] = head
    v_ref[:, 2 * LANES : 4 * LANES] = tail
    v_ref[:, 4 * LANES :] = head
    place = lax.broadcasted_iota(jnp.int32, sides_ref.shape[1:], 0)
    before = jnp.where(place >= HALO - width_ref[1], sides_ref[0], 0.0)[:HALO]
    after = jnp.where(place < width_ref[1], sides_ref[1], 0.0)[:HALO]
    centre_head, centre_tail = split(centre_ref[...])
    for slot in range(SLOTS):
        pad[...] = jnp.zeros_like(pad)
        pad[2 * HALO * slot : 2 * HALO * slot + HALO, :] = before
        pad[2 * HALO * slot + HALO : 2 * HALO * (slot + 1), :] = after
        head, tail = split(pad[...])
        w_ref[slot] = jnp.concatenate(
            [centre_head, head, centre_head, head, centre_tail, tail], axis=0
        )


def unpack_kernel(in_ref, facet_ref, side_ref, first_ref, second_ref, *, chans, deal, senders):
    groups = chans // SLOTS
    block = deal * (chans + groups)
    odd = even_row()
    for at in range(chans + groups):
        if at < chans:
            starts = [q * chans + at for q in range(deal)]
        else:
            starts = [deal * chans + q * groups + at - chans for q in range(deal)]
        rows = jnp.concatenate([in_ref[pl.ds(s, senders, stride=block), :] for s in starts], axis=0)
        held, place = (facet_ref, at) if at < chans else (side_ref, at - chans)
        held[place] = rows
        top, bottom = rows[:EDGE], rows[FACET - EDGE :]
        first_ref[at] = jnp.where(odd, top, bottom)
        second_ref[at] = jnp.where(odd, bottom, top)


def project_kernel(facet_ref, nuc_ref, basis_ref, combined_ref, out_ref, *, chans, rank):
    for part in range(0, FACET, 32):
        rows = pl.ds(part, 32)
        total = [None] * rank
        for ch in range(chans):
            block = nuc_ref[ch, rows, :] + facet_ref[ch, rows, :]
            combined_ref[ch, rows, :] = block
            for k in range(rank):
                term = basis_ref[k, ch] * block
                total[k] = term if total[k] is None else total[k] + term
        for k in range(rank):
            out_ref[k, rows, :] = total[k]


def wavelet_kernel(
    pick_ref, facet_ref, side_ref, first_ref, second_ref, v_ref, w_ref, partial_ref, wave_ref,
    out_ref, own_ref, other_ref, squares, *, chans,
):
    core = lax.rem(spec_index(), 2)
    chips = own_ref.shape[0]
    share = own_ref.shape[1] - FACET
    for chip in range(chips):
        own_ref[chip, :FACET, :] = partial_ref[2 * chip + core]
        other_ref[chip, :FACET, :] = partial_ref[2 * chip + 1 - core]
    squares[...] = jnp.zeros_like(squares)
    groups = chans // SLOTS
    half = FACET // 2
    lane = lax.broadcasted_iota(jnp.int32, (half, LANES), 1)
    nothing = jnp.zeros((2 * LANES - EXT, 2 * LANES), jnp.bfloat16)
    sides = [
        split(jnp.concatenate([side_ref[g], first_ref[chans + g], second_ref[chans + g]], axis=0))
        for g in range(groups)
    ]
    for slot in range(SLOTS):
        taken = []
        for group in range(groups):
            ch = group * SLOTS + slot
            head, tail = split(jnp.concatenate([facet_ref[ch], first_ref[ch], second_ref[ch]], axis=0))
            side_head, side_tail = sides[group]
            taken.append(jnp.concatenate([head, side_head, tail, side_tail, head, side_head], axis=1))
        across = jnp.dot(
            jnp.concatenate(taken, axis=0), w_ref[slot], preferred_element_type=jnp.float32
        )
        for group in range(groups):
            ch = group * SLOTS + slot
            head, tail = split(across[group * EXT : (group + 1) * EXT])
            stacked = jnp.concatenate([head, nothing, head, nothing, tail, nothing], axis=0)
            both = jnp.dot(v_ref[...], stacked, preferred_element_type=jnp.float32)
            upper = jnp.where(lane < half, both[:half, :LANES], both[half:FACET, :LANES])
            coeffs = jnp.concatenate([upper, both[FACET:, LANES:]], axis=0)
            dual = wave_ref[ch] + coeffs
            out_ref[ch] = dual
            square = dual * dual
            high = jnp.tile(pick_ref[ch], (FACET // 8, 1)) == 1
            squares[:FACET, :] += jnp.where(high, 0.0, square)
            squares[FACET:, :] += jnp.where(high, square, 0.0)
    for chip in range(chips):
        first = pl.multiple_of((2 * chip + core) * share, share)
        own_ref[chip, FACET:, :] = squares[pl.ds(first, share), :]
        first = pl.multiple_of((2 * chip + 1 - core) * share, share)
        other_ref[chip, FACET:, :] = squares[pl.ds(first, share), :]


def pair_kernel(own_ref, came_ref, out_ref):
    out_ref[...] = own_ref[...] + came_ref[...]


def weigh_kernel(thresh_ref, weight_ref, parts_ref, out_ref):
    chips = parts_ref.shape[0]
    total = parts_ref[0]
    for chip in range(1, chips):
        total = total + parts_ref[chip]
    spectrum, squares = total[:FACET], total[FACET:]
    me = spec_index()
    mine = lax.broadcasted_iota(jnp.int32, thresh_ref.shape, 1) == me
    threshold = jnp.sum(jnp.where(mine, thresh_ref[...], 0.0), keepdims=True)
    singular = jnp.sqrt(jnp.sum(spectrum * spectrum, keepdims=True))
    scaled = spectrum * (1.0 - threshold / jnp.maximum(singular, threshold))
    weight = weight_ref[me]
    ratio = weight / jnp.maximum(jnp.sqrt(squares), weight)
    for chip in range(chips):
        out_ref[chip, :FACET] = scaled
        out_ref[chip, FACET:] = ratio


def finish_kernel(
    spread_ref, pick_ref, combined_ref, dual_ref, own_ref, other_ref, wave_ref, nuc_ref,
    ordered, wave, nuc, sems, *, chans, rank,
):
    core, chips = lax.rem(spec_index(), 2), own_ref.shape[0]
    for chip in range(chips):
        ordered[2 * chip + core] = own_ref[chip]
        ordered[2 * chip + 1 - core] = other_ref[chip]
    share = ordered.shape[1] - FACET
    pieces = FACET // share
    tiles = (share // 8, 8, LANES)
    copies = []
    for part in range(pieces):
        rows = pl.ds(part * share, share)
        scaled = [ordered[k, rows, :].reshape(tiles) for k in range(rank)]
        ratios = [ordered[band * pieces + part, FACET:, :].reshape(tiles) for band in range(2)]
        for ch in range(chans):
            total = spread_ref[0, ch] * scaled[0]
            for k in range(1, rank):
                total = total + spread_ref[k, ch] * scaled[k]
            nuc[ch, rows, :] = combined_ref[ch, rows, :] - total.reshape(share, LANES)
            ratio = jnp.where(jnp.broadcast_to(pick_ref[ch] == 1, tiles), ratios[1], ratios[0])
            wave[ch, rows, :] = dual_ref[ch, rows, :] * ratio.reshape(share, LANES)
        for place, (held, out) in enumerate(((nuc, nuc_ref), (wave, wave_ref))):
            copy = pltpu.make_async_copy(held.at[:, rows, :], out.at[:, rows, :], sems.at[place, part])
            copy.start()
            copies.append(copy)
    for copy in copies:
        copy.wait()


def call(kernel, name, ins, outs, operands, scratch=(), flops=0, limit=24, places=None):
    size = sum(4 * int(np.prod(o.shape)) for o in outs) + sum(4 * int(np.prod(o.shape)) for o in operands)
    return pl.pallas_call(
        kernel,
        name=name,
        in_specs=ins,
        out_specs=places or [VMEM] * len(outs),
        out_shape=outs,
        scratch_shapes=list(scratch),
        compiler_params=pltpu.CompilerParams(vmem_limit_bytes=limit * 1024 * 1024),
        cost_estimate=pl.CostEstimate(flops=flops, bytes_accessed=size, transcendentals=0),
    )(*operands)


def f32(*shape):
    return jax.ShapeDtypeStruct(shape, jnp.float32)


def bf16(*shape):
    return jax.ShapeDtypeStruct(shape, jnp.bfloat16)


def shards(primal_slab, wave_dual, nuc_dual, l21_weights, nuc_thresh, basis, band_of, margin_width):
    chans = wave_dual.shape[0]
    spec, rows, cols = (lax.axis_size(a) for a in ("spec", "frow", "fcol"))
    senders = rows * cols
    deal = primal_slab.shape[1] // rows
    rank = basis.shape[3]
    bands = l21_weights.shape[0]
    plane = ("frow", "fcol")
    local_basis = basis.reshape(chans, rank).T
    bands_here = band_of.reshape(chans)
    widths = margin_width.reshape(2)

    groups = chans // SLOTS
    block = deal * (chans + groups)
    (packed,) = call(
        functools.partial(pack_kernel, chans=chans, facet_rows=rows, facet_cols=cols, deal=deal),
        "pack", [VMEM], [f32(senders * block, LANES)],
        [primal_slab.reshape(-1, LANES)],
    )
    arrived = lax.all_to_all(
        packed.reshape(senders, block, LANES), plane, split_axis=0, concat_axis=0, tiled=True
    )
    centre, sides = column_operators()
    vertical, across, spread, pick = call(
        prepare_kernel, "prepare", [SMEM] * 3 + [VMEM] * 3,
        [bf16(3 * FACET // 2, 6 * LANES), bf16(SLOTS, 6 * LANES, 2 * LANES),
         f32(rank, chans, 8, LANES), jax.ShapeDtypeStruct((chans, 8, LANES), jnp.int32)],
        [widths, local_basis, bands_here, jnp.asarray(row_operator()), jnp.asarray(centre), jnp.asarray(sides)],
        scratch=[pltpu.VMEM((LANES, 2 * LANES), jnp.float32)],
    )
    strip = f32(chans + groups, EDGE, LANES)
    facet, side, first, second = call(
        functools.partial(unpack_kernel, chans=chans, deal=deal, senders=senders),
        "unpack", [VMEM],
        [f32(chans, FACET, LANES), f32(groups, FACET, LANES), strip, strip],
        [arrived.reshape(-1, LANES)],
    )
    inward = [(i, i - 1 if i % 2 == 0 else i + 1) for i in range(1, rows - 1)]
    first = lax.ppermute(first, "frow", inward)
    second = lax.ppermute(second, "frow", [(i, i ^ 1) for i in range(rows)])
    combined, partial = call(
        functools.partial(project_kernel, chans=chans, rank=rank),
        "project", [VMEM, VMEM, SMEM],
        [f32(chans, FACET, LANES), f32(rank, FACET, LANES)],
        [facet, nuc_dual, local_basis],
        flops=2 * chans * rank * FACET * LANES,
    )
    share = bands * FACET // spec
    chips = spec // 2
    chunks = f32(chips, FACET + share, LANES)
    dual_sum, own, other = call(
        functools.partial(wavelet_kernel, chans=chans),
        "wavelet", [VMEM] * 9,
        [f32(chans, FACET, LANES), chunks, chunks],
        [pick, facet, side, first, second, vertical, across, partial, wave_dual],
        scratch=[
            pltpu.VMEM((bands * FACET, LANES), jnp.float32),
        ],
        flops=2 * chans * 3 * 192 * 256 * 600,
    )

    def swap(values):
        return lax.ppermute(values, "spec", [(i, i ^ 1) for i in range(spec)])

    def across_chips(values):
        cores = [list(range(core, spec, 2)) for core in range(2)]
        return lax.all_to_all(
            values, "spec", split_axis=0, concat_axis=0, tiled=True, axis_index_groups=cores
        )

    (sums,) = call(pair_kernel, "pair", [VMEM, VMEM], [chunks], [own, swap(other)])
    (weighed,) = call(
        weigh_kernel, "weigh", [VMEM] * 3, [chunks],
        [nuc_thresh.reshape(1, rank), l21_weights.reshape(spec, share, LANES), across_chips(sums)],
    )
    own = across_chips(weighed)
    wave_new, nuc_new = call(
        functools.partial(finish_kernel, chans=chans, rank=rank),
        "finish", [VMEM] * 6,
        [f32(chans, FACET, LANES), f32(chans, FACET, LANES)],
        [spread, pick, combined, dual_sum, own, swap(own)],
        scratch=[
            pltpu.VMEM((spec, FACET + share, LANES), jnp.float32),
            pltpu.VMEM((chans, FACET, LANES), jnp.float32),
            pltpu.VMEM((chans, FACET, LANES), jnp.float32),
            pltpu.SemaphoreType.DMA((2, FACET // share)),
        ],
        flops=2 * chans * rank * FACET * LANES,
        places=[HBM, HBM],
    )
    return (wave_new, nuc_new)


def solution(mesh):
    return jax.shard_map(
        shards,
        mesh=mesh,
        in_specs=(
            P("spec", None, "frow", "fcol", None),
            P("spec", "frow", "fcol"),
            P("spec", "frow", "fcol"),
            P(None, "frow", "fcol"),
            P("frow", "fcol", None),
            P("frow", "fcol", "spec", None),
            P("frow", "fcol", "spec"),
            P("frow", "fcol", None),
        ),
        out_specs=(P("spec", "frow", "fcol"), P("spec", "frow", "fcol")),
        check_vma=False,
    )
```

```python
import functools

import jax
import jax.numpy as jnp
import numpy as np
from jax import lax
from jax.experimental import pallas as pl
from jax.experimental.pallas import tpu as pltpu
from jax.sharding import PartitionSpec as P

HALO = 21
EDGE = 24
SLOTS = 3
LANES = 128
FACET = 128
EXT = FACET + 2 * EDGE
VMEM = pl.BlockSpec(memory_space=pltpu.VMEM)
SMEM = pl.BlockSpec(memory_space=pltpu.SMEM)
HBM = pl.BlockSpec(memory_space=pltpu.HBM)

low_taps = [
    -0.00011747678400228192,
    0.0006754494059985568,
    -0.0003917403729959771,
    -0.00487035299301066,
    0.008746094047015655,
    0.013981027917015516,
    -0.04408825393106472,
    -0.01736930100202211,
    0.128747426620186,
    0.00047248457399797254,
    -0.2840155429624281,
    -0.015829105256023893,
    0.5853546836548691,
    0.6756307362980128,
    0.3128715909144659,
    0.05441584224308161,
]
tap_lag = 7
high_taps = [(-1.0) ** place * low_taps[15 - place] for place in range(16)]


def filter_matrix(in_length, taps, first, count):
    matrix = np.zeros((count, in_length))
    for out in range(count):
        matrix[out, 2 * (out + first) : 2 * (out + first) + 16] = taps
    return matrix


@functools.cache
def operators():
    length = FACET + 2 * HALO
    half, quarter = FACET // 2, FACET // 4
    low_all = filter_matrix(length, low_taps, 0, half + 14)
    high = filter_matrix(length, high_taps, tap_lag, half)
    low = low_all[tap_lag : tap_lag + half]
    coarse = np.concatenate(
        [
            filter_matrix(half + 14, low_taps, 0, quarter) @ low_all,
            filter_matrix(half + 14, high_taps, 0, quarter) @ low_all,
        ]
    )
    return coarse, low, high


def row_operator():
    whole = np.concatenate(operators())
    placed = np.zeros((2, whole.shape[0], 2 * LANES), np.float32)
    placed[:, :, :FACET] = whole[:, HALO : HALO + FACET]
    above, below = whole[:, :HALO], whole[:, HALO + FACET :]
    placed[0, :, FACET : FACET + HALO] = below
    placed[0, :, EXT - HALO : EXT] = above
    placed[1, :, FACET + EDGE - HALO : FACET + EDGE] = above
    placed[1, :, FACET + EDGE : FACET + EDGE + HALO] = below
    return placed


def column_operators():
    coarse, low, high = operators()
    whole = np.concatenate([coarse, high, low, high]).T.astype(np.float32)
    sides = np.zeros((2, EDGE, 2 * LANES), np.float32)
    sides[0, :HALO] = whole[:HALO]
    sides[1, :HALO] = whole[HALO + FACET :]
    return whole[HALO : HALO + FACET], sides


def spec_index():
    return lax.axis_index("spec").astype(jnp.int32)


def even_row():
    return lax.rem(lax.axis_index("frow").astype(jnp.int32), 2) == 0


def split(values):
    head = values.astype(jnp.bfloat16)
    return head, (values - head.astype(jnp.float32)).astype(jnp.bfloat16)


def pack_kernel(rows_ref, out_ref, *, chans, facet_rows, facet_cols, deal):
    block = deal * (chans + chans // SLOTS)
    per_chan = deal * facet_rows * facet_cols
    for i in range(facet_rows):
        for q in range(deal):
            for j in range(facet_cols):
                first = (deal * i + q) * facet_cols + j
                out_ref[pl.ds((i * facet_cols + j) * block + q * chans, chans), :] = rows_ref[
                    pl.ds(first, chans, stride=per_chan), :
                ]
    lane = lax.broadcasted_iota(jnp.int32, (per_chan, LANES), 1)
    column = lax.broadcasted_iota(jnp.int32, (per_chan, LANES), 0) % facet_cols
    for group in range(chans // SLOTS):
        left = jnp.zeros((per_chan, LANES), jnp.float32)
        right = jnp.zeros((per_chan, LANES), jnp.float32)
        on_left = lane < 0
        for slot in range(SLOTS):
            rows = rows_ref[pl.ds((group * SLOTS + slot) * per_chan, per_chan), :]
            start = 2 * HALO * slot
            here = (lane >= start) & (lane < start + HALO)
            on_left = on_left | here
            left = jnp.where(here, pltpu.roll(rows, (start + HALO) % LANES, 1), left)
            here = (lane >= start + HALO) & (lane < start + 2 * HALO)
            right = jnp.where(here, pltpu.roll(rows, start + HALO, 1), right)
        left = jnp.where(column > 0, pltpu.roll(left, 1, 0), 0.0)
        right = jnp.where(column < facet_cols - 1, pltpu.roll(right, per_chan - 1, 0), 0.0)
        sides = jnp.where(on_left, left, right)
        for i in range(facet_rows):
            for q in range(deal):
                first = (deal * i + q) * facet_cols
                place = i * facet_cols * block + deal * chans + q * (chans // SLOTS) + group
                out_ref[pl.ds(place, facet_cols, stride=block), :] = sides[first : first + facet_cols]


def prepare_kernel(
    width_ref, basis_ref, band_ref, rows_ref, centre_ref, sides_ref,
    v_ref, w_ref, spread_ref, pick_ref, pad,
):
    rank, chans = basis_ref.shape
    for ch in range(chans):
        pick_ref[ch] = jnp.full((8, LANES), band_ref[ch], jnp.int32)
        for k in range(rank):
            spread_ref[k, ch] = jnp.full((8, LANES), basis_ref[k, ch], jnp.float32)
    odd = even_row().astype(jnp.int32)
    lane = lax.broadcasted_iota(jnp.int32, rows_ref.shape[1:], 1)
    first = jnp.where(odd == 1, FACET + EDGE - width_ref[0], EXT - width_ref[0])
    last = jnp.where(odd == 1, FACET + EDGE, FACET) + width_ref[0]
    above = (lane >= first) & (lane < first + width_ref[0])
    below = (lane >= last - width_ref[0]) & (lane < last)
    head, tail = split(jnp.where((lane < FACET) | above | below, rows_ref[odd], 0.0))
    v_ref[:, : 2 * LANES] = head
    v_ref[:, 2 * LANES : 4 * LANES] = tail
    v_ref[:, 4 * LANES :] = head
    place = lax.broadcasted_iota(jnp.int32, sides_ref.shape[1:], 0)
    before = jnp.where(place >= HALO - width_ref[1], sides_ref[0], 0.0)[:HALO]
    after = jnp.where(place < width_ref[1], sides_ref[1], 0.0)[:HALO]
    centre_head, centre_tail = split(centre_ref[...])
    for slot in range(SLOTS):
        pad[...] = jnp.zeros_like(pad)
        pad[2 * HALO * slot : 2 * HALO * slot + HALO, :] = before
        pad[2 * HALO * slot + HALO : 2 * HALO * (slot + 1), :] = after
        head, tail = split(pad[...])
        w_ref[slot] = jnp.concatenate(
            [centre_head, head, centre_head, head, centre_tail, tail], axis=0
        )


def unpack_kernel(in_ref, facet_ref, side_ref, first_ref, second_ref, *, chans, deal, senders):
    groups = chans // SLOTS
    block = deal * (chans + groups)
    odd = even_row()
    for at in range(chans + groups):
        if at < chans:
            starts = [q * chans + at for q in range(deal)]
        else:
            starts = [deal * chans + q * groups + at - chans for q in range(deal)]
        rows = jnp.concatenate([in_ref[pl.ds(s, senders, stride=block), :] for s in starts], axis=0)
        held, place = (facet_ref, at) if at < chans else (side_ref, at - chans)
        held[place] = rows
        top, bottom = rows[:EDGE], rows[FACET - EDGE :]
        first_ref[at] = jnp.where(odd, top, bottom)
        second_ref[at] = jnp.where(odd, bottom, top)


def project_kernel(facet_ref, nuc_ref, basis_ref, combined_ref, out_ref, *, chans, rank):
    for part in range(0, FACET, 32):
        rows = pl.ds(part, 32)
        total = [None] * rank
        for ch in range(chans):
            block = nuc_ref[ch, rows, :] + facet_ref[ch, rows, :]
            combined_ref[ch, rows, :] = block
            for k in range(rank):
                term = basis_ref[k, ch] * block
                total[k] = term if total[k] is None else total[k] + term
        for k in range(rank):
            out_ref[k, rows, :] = total[k]


def along_columns(chans, slot, rows, sides, w_ref):
    taken = []
    for group in range(chans // SLOTS):
        head, tail = split(rows(group * SLOTS + slot))
        side_head, side_tail = sides[group]
        taken.append(jnp.concatenate([head, side_head, tail, side_tail, head, side_head], axis=1))
    return jnp.dot(jnp.concatenate(taken, axis=0), w_ref[slot], preferred_element_type=jnp.float32)


def columns_kernel(facet_ref, side_ref, w_ref, out_ref, *, chans):
    sides = [split(side_ref[group]) for group in range(chans // SLOTS)]
    for slot in range(SLOTS):
        across = along_columns(chans, slot, lambda ch: facet_ref[ch], sides, w_ref)
        for group in range(chans // SLOTS):
            head, tail = split(across[group * FACET : (group + 1) * FACET])
            out_ref[group * SLOTS + slot, 0] = head
            out_ref[group * SLOTS + slot, 1] = tail


def wavelet_kernel(
    pick_ref, columns_ref, first_ref, second_ref, v_ref, w_ref, partial_ref, wave_ref,
    out_ref, own_ref, other_ref, squares, *, chans,
):
    core = lax.rem(spec_index(), 2)
    chips = own_ref.shape[0]
    share = own_ref.shape[1] - FACET
    for chip in range(chips):
        own_ref[chip, :FACET, :] = partial_ref[2 * chip + core]
        other_ref[chip, :FACET, :] = partial_ref[2 * chip + 1 - core]
    squares[...] = jnp.zeros_like(squares)
    groups = chans // SLOTS
    half = FACET // 2
    lane = lax.broadcasted_iota(jnp.int32, (half, LANES), 1)
    nothing = jnp.zeros((2 * LANES - EXT, 2 * LANES), jnp.bfloat16)
    margin = EXT - FACET

    def margins(ch):
        return jnp.concatenate([first_ref[ch], second_ref[ch]], axis=0)

    sides = [split(margins(chans + group)) for group in range(groups)]
    for slot in range(SLOTS):
        across = along_columns(chans, slot, margins, sides, w_ref)
        for group in range(groups):
            ch = group * SLOTS + slot
            head, tail = split(across[group * margin : (group + 1) * margin])
            head = [columns_ref[ch, 0], head, nothing]
            stacked = jnp.concatenate(head + head + [columns_ref[ch, 1], tail, nothing], axis=0)
            both = jnp.dot(v_ref[...], stacked, preferred_element_type=jnp.float32)
            upper = jnp.where(lane < half, both[:half, :LANES], both[half:FACET, :LANES])
            coeffs = jnp.concatenate([upper, both[FACET:, LANES:]], axis=0)
            dual = wave_ref[ch] + coeffs
            out_ref[ch] = dual
            square = dual * dual
            high = jnp.tile(pick_ref[ch], (FACET // 8, 1)) == 1
            squares[:FACET, :] += jnp.where(high, 0.0, square)
            squares[FACET:, :] += jnp.where(high, square, 0.0)
    for chip in range(chips):
        first = pl.multiple_of((2 * chip + core) * share, share)
        own_ref[chip, FACET:, :] = squares[pl.ds(first, share), :]
        first = pl.multiple_of((2 * chip + 1 - core) * share, share)
        other_ref[chip, FACET:, :] = squares[pl.ds(first, share), :]


def pair_kernel(own_ref, came_ref, out_ref):
    out_ref[...] = own_ref[...] + came_ref[...]


def weigh_kernel(thresh_ref, weight_ref, parts_ref, out_ref):
    chips = parts_ref.shape[0]
    total = parts_ref[0]
    for chip in range(1, chips):
        total = total + parts_ref[chip]
    spectrum, squares = total[:FACET], total[FACET:]
    me = spec_index()
    mine = lax.broadcasted_iota(jnp.int32, thresh_ref.shape, 1) == me
    threshold = jnp.sum(jnp.where(mine, thresh_ref[...], 0.0), keepdims=True)
    singular = jnp.sqrt(jnp.sum(spectrum * spectrum, keepdims=True))
    scaled = spectrum * (1.0 - threshold / jnp.maximum(singular, threshold))
    weight = weight_ref[me]
    ratio = weight / jnp.maximum(jnp.sqrt(squares), weight)
    for chip in range(chips):
        out_ref[chip, :FACET] = scaled
        out_ref[chip, FACET:] = ratio


def finish_kernel(
    spread_ref, pick_ref, combined_ref, dual_ref, own_ref, other_ref, wave_ref, nuc_ref,
    ordered, wave, nuc, sems, *, chans, rank,
):
    core, chips = lax.rem(spec_index(), 2), own_ref.shape[0]
    for chip in range(chips):
        ordered[2 * chip + core] = own_ref[chip]
        ordered[2 * chip + 1 - core] = other_ref[chip]
    share = ordered.shape[1] - FACET
    pieces = FACET // share
    tiles = (share // 8, 8, LANES)
    copies = []
    for part in range(pieces):
        rows = pl.ds(part * share, share)
        scaled = [ordered[k, rows, :].reshape(tiles) for k in range(rank)]
        ratios = [ordered[band * pieces + part, FACET:, :].reshape(tiles) for band in range(2)]
        for ch in range(chans):
            total = spread_ref[0, ch] * scaled[0]
            for k in range(1, rank):
                total = total + spread_ref[k, ch] * scaled[k]
            nuc[ch, rows, :] = combined_ref[ch, rows, :] - total.reshape(share, LANES)
            ratio = jnp.where(jnp.broadcast_to(pick_ref[ch] == 1, tiles), ratios[1], ratios[0])
            wave[ch, rows, :] = dual_ref[ch, rows, :] * ratio.reshape(share, LANES)
        for place, (held, out) in enumerate(((nuc, nuc_ref), (wave, wave_ref))):
            copy = pltpu.make_async_copy(held.at[:, rows, :], out.at[:, rows, :], sems.at[place, part])
            copy.start()
            copies.append(copy)
    for copy in copies:
        copy.wait()


def call(kernel, name, ins, outs, operands, scratch=(), flops=0, limit=24, places=None):
    size = sum(4 * int(np.prod(o.shape)) for o in outs) + sum(4 * int(np.prod(o.shape)) for o in operands)
    return pl.pallas_call(
        kernel,
        name=name,
        in_specs=ins,
        out_specs=places or [VMEM] * len(outs),
        out_shape=outs,
        scratch_shapes=list(scratch),
        compiler_params=pltpu.CompilerParams(vmem_limit_bytes=limit * 1024 * 1024),
        cost_estimate=pl.CostEstimate(flops=flops, bytes_accessed=size, transcendentals=0),
    )(*operands)


def f32(*shape):
    return jax.ShapeDtypeStruct(shape, jnp.float32)


def bf16(*shape):
    return jax.ShapeDtypeStruct(shape, jnp.bfloat16)


def shards(primal_slab, wave_dual, nuc_dual, l21_weights, nuc_thresh, basis, band_of, margin_width):
    chans = wave_dual.shape[0]
    spec, rows, cols = (lax.axis_size(a) for a in ("spec", "frow", "fcol"))
    senders = rows * cols
    deal = primal_slab.shape[1] // rows
    rank = basis.shape[3]
    bands = l21_weights.shape[0]
    plane = ("frow", "fcol")
    local_basis = basis.reshape(chans, rank).T
    bands_here = band_of.reshape(chans)
    widths = margin_width.reshape(2)

    groups = chans // SLOTS
    block = deal * (chans + groups)
    (packed,) = call(
        functools.partial(pack_kernel, chans=chans, facet_rows=rows, facet_cols=cols, deal=deal),
        "pack", [VMEM], [f32(senders * block, LANES)],
        [primal_slab.reshape(-1, LANES)],
    )
    arrived = lax.all_to_all(
        packed.reshape(senders, block, LANES), plane, split_axis=0, concat_axis=0, tiled=True
    )
    centre, sides = column_operators()
    vertical, across, spread, pick = call(
        prepare_kernel, "prepare", [SMEM] * 3 + [VMEM] * 3,
        [bf16(3 * FACET // 2, 6 * LANES), bf16(SLOTS, 6 * LANES, 2 * LANES),
         f32(rank, chans, 8, LANES), jax.ShapeDtypeStruct((chans, 8, LANES), jnp.int32)],
        [widths, local_basis, bands_here, jnp.asarray(row_operator()), jnp.asarray(centre), jnp.asarray(sides)],
        scratch=[pltpu.VMEM((LANES, 2 * LANES), jnp.float32)],
    )
    strip = f32(chans + groups, EDGE, LANES)
    facet, side, first, second = call(
        functools.partial(unpack_kernel, chans=chans, deal=deal, senders=senders),
        "unpack", [VMEM],
        [f32(chans, FACET, LANES), f32(groups, FACET, LANES), strip, strip],
        [arrived.reshape(-1, LANES)],
    )
    inward = [(i, i - 1 if i % 2 == 0 else i + 1) for i in range(1, rows - 1)]
    first = lax.ppermute(first, "frow", inward)
    second = lax.ppermute(second, "frow", [(i, i ^ 1) for i in range(rows)])
    combined, partial = call(
        functools.partial(project_kernel, chans=chans, rank=rank),
        "project", [VMEM, VMEM, SMEM],
        [f32(chans, FACET, LANES), f32(rank, FACET, LANES)],
        [facet, nuc_dual, local_basis],
        flops=2 * chans * rank * FACET * LANES,
    )
    share = bands * FACET // spec
    chips = spec // 2
    chunks = f32(chips, FACET + share, LANES)
    (columns,) = call(
        functools.partial(columns_kernel, chans=chans),
        "columns", [VMEM] * 3, [bf16(chans, 2, FACET, 2 * LANES)], [facet, side, across],
        flops=2 * chans * 3 * 128 * 256 * 256,
    )
    dual_sum, own, other = call(
        functools.partial(wavelet_kernel, chans=chans),
        "wavelet", [VMEM] * 8,
        [f32(chans, FACET, LANES), chunks, chunks],
        [pick, columns, first, second, vertical, across, partial, wave_dual],
        scratch=[
            pltpu.VMEM((bands * FACET, LANES), jnp.float32),
        ],
        flops=2 * chans * 3 * 192 * 256 * 600,
    )

    def swap(values):
        return lax.ppermute(values, "spec", [(i, i ^ 1) for i in range(spec)])

    def across_chips(values):
        cores = [list(range(core, spec, 2)) for core in range(2)]
        return lax.all_to_all(
            values, "spec", split_axis=0, concat_axis=0, tiled=True, axis_index_groups=cores
        )

    (sums,) = call(pair_kernel, "pair", [VMEM, VMEM], [chunks], [own, swap(other)])
    (weighed,) = call(
        weigh_kernel, "weigh", [VMEM] * 3, [chunks],
        [nuc_thresh.reshape(1, rank), l21_weights.reshape(spec, share, LANES), across_chips(sums)],
    )
    own = across_chips(weighed)
    wave_new, nuc_new = call(
        functools.partial(finish_kernel, chans=chans, rank=rank),
        "finish", [VMEM] * 6,
        [f32(chans, FACET, LANES), f32(chans, FACET, LANES)],
        [spread, pick, combined, dual_sum, own, swap(own)],
        scratch=[
            pltpu.VMEM((spec, FACET + share, LANES), jnp.float32),
            pltpu.VMEM((chans, FACET, LANES), jnp.float32),
            pltpu.VMEM((chans, FACET, LANES), jnp.float32),
            pltpu.SemaphoreType.DMA((2, FACET // share)),
        ],
        flops=2 * chans * rank * FACET * LANES,
        places=[HBM, HBM],
    )
    return (wave_new, nuc_new)


def solution(mesh):
    return jax.shard_map(
        shards,
        mesh=mesh,
        in_specs=(
            P("spec", None, "frow", "fcol", None),
            P("spec", "frow", "fcol"),
            P("spec", "frow", "fcol"),
            P(None, "frow", "fcol"),
            P("frow", "fcol", None),
            P("frow", "fcol", "spec", None),
            P("frow", "fcol", "spec"),
            P("frow", "fcol", None),
        ),
        out_specs=(P("spec", "frow", "fcol"), P("spec", "frow", "fcol")),
        check_vma=False,
    )
```

```python
import functools

import jax
import jax.numpy as jnp
import numpy as np
from jax import lax
from jax.experimental import pallas as pl
from jax.experimental.pallas import tpu as pltpu
from jax.sharding import PartitionSpec as P

HALO = 21
EDGE = 24
SLOTS = 3
LANES = 128
FACET = 128
EXT = FACET + 2 * EDGE
VMEM = pl.BlockSpec(memory_space=pltpu.VMEM)
SMEM = pl.BlockSpec(memory_space=pltpu.SMEM)
HBM = pl.BlockSpec(memory_space=pltpu.HBM)

low_taps = [
    -0.00011747678400228192,
    0.0006754494059985568,
    -0.0003917403729959771,
    -0.00487035299301066,
    0.008746094047015655,
    0.013981027917015516,
    -0.04408825393106472,
    -0.01736930100202211,
    0.128747426620186,
    0.00047248457399797254,
    -0.2840155429624281,
    -0.015829105256023893,
    0.5853546836548691,
    0.6756307362980128,
    0.3128715909144659,
    0.05441584224308161,
]
tap_lag = 7
high_taps = [(-1.0) ** place * low_taps[15 - place] for place in range(16)]


def filter_matrix(in_length, taps, first, count):
    matrix = np.zeros((count, in_length))
    for out in range(count):
        matrix[out, 2 * (out + first) : 2 * (out + first) + 16] = taps
    return matrix


@functools.cache
def operators():
    length = FACET + 2 * HALO
    half, quarter = FACET // 2, FACET // 4
    low_all = filter_matrix(length, low_taps, 0, half + 14)
    high = filter_matrix(length, high_taps, tap_lag, half)
    low = low_all[tap_lag : tap_lag + half]
    coarse = np.concatenate(
        [
            filter_matrix(half + 14, low_taps, 0, quarter) @ low_all,
            filter_matrix(half + 14, high_taps, 0, quarter) @ low_all,
        ]
    )
    return coarse, low, high


def row_operator():
    whole = np.concatenate(operators())
    placed = np.zeros((2, whole.shape[0], 2 * LANES), np.float32)
    placed[:, :, :FACET] = whole[:, HALO : HALO + FACET]
    above, below = whole[:, :HALO], whole[:, HALO + FACET :]
    placed[0, :, FACET : FACET + HALO] = below
    placed[0, :, EXT - HALO : EXT] = above
    placed[1, :, FACET + EDGE - HALO : FACET + EDGE] = above
    placed[1, :, FACET + EDGE : FACET + EDGE + HALO] = below
    return placed


def column_operators():
    coarse, low, high = operators()
    whole = np.concatenate([coarse, high, low, high]).T.astype(np.float32)
    sides = np.zeros((2, EDGE, 2 * LANES), np.float32)
    sides[0, :HALO] = whole[:HALO]
    sides[1, :HALO] = whole[HALO + FACET :]
    return whole[HALO : HALO + FACET], sides


def spec_index():
    return lax.axis_index("spec").astype(jnp.int32)


def even_row():
    return lax.rem(lax.axis_index("frow").astype(jnp.int32), 2) == 0


def split(values):
    head = values.astype(jnp.bfloat16)
    return head, (values - head.astype(jnp.float32)).astype(jnp.bfloat16)


def pack_kernel(rows_ref, out_ref, *, chans, facet_rows, facet_cols, deal):
    block = deal * (chans + chans // SLOTS)
    per_chan = deal * facet_rows * facet_cols
    for i in range(facet_rows):
        for q in range(deal):
            for j in range(facet_cols):
                first = (deal * i + q) * facet_cols + j
                out_ref[pl.ds((j * facet_rows + i) * block + q * chans, chans), :] = rows_ref[
                    pl.ds(first, chans, stride=per_chan), :
                ]
    lane = lax.broadcasted_iota(jnp.int32, (per_chan, LANES), 1)
    column = lax.broadcasted_iota(jnp.int32, (per_chan, LANES), 0) % facet_cols
    for group in range(chans // SLOTS):
        left = jnp.zeros((per_chan, LANES), jnp.float32)
        right = jnp.zeros((per_chan, LANES), jnp.float32)
        on_left = lane < 0
        for slot in range(SLOTS):
            rows = rows_ref[pl.ds((group * SLOTS + slot) * per_chan, per_chan), :]
            start = 2 * HALO * slot
            here = (lane >= start) & (lane < start + HALO)
            on_left = on_left | here
            left = jnp.where(here, pltpu.roll(rows, (start + HALO) % LANES, 1), left)
            here = (lane >= start + HALO) & (lane < start + 2 * HALO)
            right = jnp.where(here, pltpu.roll(rows, start + HALO, 1), right)
        left = jnp.where(column > 0, pltpu.roll(left, 1, 0), 0.0)
        right = jnp.where(column < facet_cols - 1, pltpu.roll(right, per_chan - 1, 0), 0.0)
        sides = jnp.where(on_left, left, right)
        for i in range(facet_rows):
            for q in range(deal):
                first = (deal * i + q) * facet_cols
                place = i * block + deal * chans + q * (chans // SLOTS) + group
                out_ref[pl.ds(place, facet_cols, stride=facet_rows * block), :] = sides[first : first + facet_cols]


def prepare_kernel(
    width_ref, basis_ref, band_ref, rows_ref, centre_ref, sides_ref,
    v_ref, w_ref, spread_ref, pick_ref, pad,
):
    rank, chans = basis_ref.shape
    for ch in range(chans):
        pick_ref[ch] = jnp.full((8, LANES), band_ref[ch], jnp.int32)
        for k in range(rank):
            spread_ref[k, ch] = jnp.full((8, LANES), basis_ref[k, ch], jnp.float32)
    odd = even_row().astype(jnp.int32)
    lane = lax.broadcasted_iota(jnp.int32, rows_ref.shape[1:], 1)
    first = jnp.where(odd == 1, FACET + EDGE - width_ref[0], EXT - width_ref[0])
    last = jnp.where(odd == 1, FACET + EDGE, FACET) + width_ref[0]
    above = (lane >= first) & (lane < first + width_ref[0])
    below = (lane >= last - width_ref[0]) & (lane < last)
    head, tail = split(jnp.where((lane < FACET) | above | below, rows_ref[odd], 0.0))
    v_ref[:, : 2 * LANES] = head
    v_ref[:, 2 * LANES : 4 * LANES] = tail
    v_ref[:, 4 * LANES :] = head
    place = lax.broadcasted_iota(jnp.int32, sides_ref.shape[1:], 0)
    before = jnp.where(place >= HALO - width_ref[1], sides_ref[0], 0.0)[:HALO]
    after = jnp.where(place < width_ref[1], sides_ref[1], 0.0)[:HALO]
    centre_head, centre_tail = split(centre_ref[...])
    for slot in range(SLOTS):
        pad[...] = jnp.zeros_like(pad)
        pad[2 * HALO * slot : 2 * HALO * slot + HALO, :] = before
        pad[2 * HALO * slot + HALO : 2 * HALO * (slot + 1), :] = after
        head, tail = split(pad[...])
        w_ref[slot] = jnp.concatenate(
            [centre_head, head, centre_head, head, centre_tail, tail], axis=0
        )


def unpack_kernel(
    in_ref, facet_ref, side_ref, first_ref, second_ref, *, chans, deal, facet_rows, facet_cols
):
    groups = chans // SLOTS
    block = deal * (chans + groups)
    odd = even_row()
    for at in range(chans + groups):
        if at < chans:
            starts = [q * chans + at for q in range(deal)]
        else:
            starts = [deal * chans + q * groups + at - chans for q in range(deal)]
        rows = [
            in_ref[pl.ds(r * block + start, facet_cols, stride=facet_rows * block), :]
            for start in starts
            for r in range(facet_rows)
        ]
        rows = jnp.concatenate(rows, axis=0)
        held, place = (facet_ref, at) if at < chans else (side_ref, at - chans)
        held[place] = rows
        top, bottom = rows[:EDGE], rows[FACET - EDGE :]
        first_ref[at] = jnp.where(odd, top, bottom)
        second_ref[at] = jnp.where(odd, bottom, top)


def project_kernel(facet_ref, nuc_ref, basis_ref, combined_ref, out_ref, *, chans, rank):
    for part in range(0, FACET, 32):
        rows = pl.ds(part, 32)
        total = [None] * rank
        for ch in range(chans):
            block = nuc_ref[ch, rows, :] + facet_ref[ch, rows, :]
            combined_ref[ch, rows, :] = block
            for k in range(rank):
                term = basis_ref[k, ch] * block
                total[k] = term if total[k] is None else total[k] + term
        for k in range(rank):
            out_ref[k, rows, :] = total[k]


def along_columns(chans, slot, rows, sides, w_ref):
    taken = []
    for group in range(chans // SLOTS):
        head, tail = split(rows(group * SLOTS + slot))
        side_head, side_tail = sides[group]
        taken.append(jnp.concatenate([head, side_head, tail, side_tail, head, side_head], axis=1))
    return jnp.dot(jnp.concatenate(taken, axis=0), w_ref[slot], preferred_element_type=jnp.float32)


def columns_kernel(facet_ref, side_ref, w_ref, out_ref, *, chans):
    sides = [split(side_ref[group]) for group in range(chans // SLOTS)]
    for slot in range(SLOTS):
        across = along_columns(chans, slot, lambda ch: facet_ref[ch], sides, w_ref)
        for group in range(chans // SLOTS):
            head, tail = split(across[group * FACET : (group + 1) * FACET])
            out_ref[group * SLOTS + slot, 0] = head
            out_ref[group * SLOTS + slot, 1] = tail


def wavelet_kernel(
    pick_ref, columns_ref, first_ref, second_ref, v_ref, w_ref, partial_ref, wave_ref,
    out_ref, own_ref, other_ref, squares, *, chans,
):
    core = lax.rem(spec_index(), 2)
    chips = own_ref.shape[0]
    share = own_ref.shape[1] - FACET
    for chip in range(chips):
        own_ref[chip, :FACET, :] = partial_ref[2 * chip + core]
        other_ref[chip, :FACET, :] = partial_ref[2 * chip + 1 - core]
    squares[...] = jnp.zeros_like(squares)
    groups = chans // SLOTS
    half = FACET // 2
    lane = lax.broadcasted_iota(jnp.int32, (half, LANES), 1)
    nothing = jnp.zeros((2 * LANES - EXT, 2 * LANES), jnp.bfloat16)
    margin = EXT - FACET

    def margins(ch):
        return jnp.concatenate([first_ref[ch], second_ref[ch]], axis=0)

    sides = [split(margins(chans + group)) for group in range(groups)]
    for slot in range(SLOTS):
        across = along_columns(chans, slot, margins, sides, w_ref)
        for group in range(groups):
            ch = group * SLOTS + slot
            head, tail = split(across[group * margin : (group + 1) * margin])
            head = [columns_ref[ch, 0], head, nothing]
            stacked = jnp.concatenate(head + head + [columns_ref[ch, 1], tail, nothing], axis=0)
            both = jnp.dot(v_ref[...], stacked, preferred_element_type=jnp.float32)
            upper = jnp.where(lane < half, both[:half, :LANES], both[half:FACET, :LANES])
            coeffs = jnp.concatenate([upper, both[FACET:, LANES:]], axis=0)
            dual = wave_ref[ch] + coeffs
            out_ref[ch] = dual
            square = dual * dual
            high = jnp.tile(pick_ref[ch], (FACET // 8, 1)) == 1
            squares[:FACET, :] += jnp.where(high, 0.0, square)
            squares[FACET:, :] += jnp.where(high, square, 0.0)
    for chip in range(chips):
        first = pl.multiple_of((2 * chip + core) * share, share)
        own_ref[chip, FACET:, :] = squares[pl.ds(first, share), :]
        first = pl.multiple_of((2 * chip + 1 - core) * share, share)
        other_ref[chip, FACET:, :] = squares[pl.ds(first, share), :]


def pair_kernel(own_ref, came_ref, out_ref):
    out_ref[...] = own_ref[...] + came_ref[...]


def weigh_kernel(thresh_ref, weight_ref, parts_ref, out_ref):
    chips = parts_ref.shape[0]
    total = parts_ref[0]
    for chip in range(1, chips):
        total = total + parts_ref[chip]
    spectrum, squares = total[:FACET], total[FACET:]
    me = spec_index()
    mine = lax.broadcasted_iota(jnp.int32, thresh_ref.shape, 1) == me
    threshold = jnp.sum(jnp.where(mine, thresh_ref[...], 0.0), keepdims=True)
    singular = jnp.sqrt(jnp.sum(spectrum * spectrum, keepdims=True))
    scaled = spectrum * (1.0 - threshold / jnp.maximum(singular, threshold))
    weight = weight_ref[me]
    ratio = weight / jnp.maximum(jnp.sqrt(squares), weight)
    for chip in range(chips):
        out_ref[chip, :FACET] = scaled
        out_ref[chip, FACET:] = ratio


def finish_kernel(
    spread_ref, pick_ref, combined_ref, dual_ref, own_ref, other_ref, wave_ref, nuc_ref,
    ordered, wave, nuc, sems, *, chans, rank,
):
    core, chips = lax.rem(spec_index(), 2), own_ref.shape[0]
    for chip in range(chips):
        ordered[2 * chip + core] = own_ref[chip]
        ordered[2 * chip + 1 - core] = other_ref[chip]
    share = ordered.shape[1] - FACET
    pieces = FACET // share
    tiles = (share // 8, 8, LANES)
    copies = []
    for part in range(pieces):
        rows = pl.ds(part * share, share)
        scaled = [ordered[k, rows, :].reshape(tiles) for k in range(rank)]
        ratios = [ordered[band * pieces + part, FACET:, :].reshape(tiles) for band in range(2)]
        for ch in range(chans):
            total = spread_ref[0, ch] * scaled[0]
            for k in range(1, rank):
                total = total + spread_ref[k, ch] * scaled[k]
            nuc[ch, rows, :] = combined_ref[ch, rows, :] - total.reshape(share, LANES)
            ratio = jnp.where(jnp.broadcast_to(pick_ref[ch] == 1, tiles), ratios[1], ratios[0])
            wave[ch, rows, :] = dual_ref[ch, rows, :] * ratio.reshape(share, LANES)
        for place, (held, out) in enumerate(((nuc, nuc_ref), (wave, wave_ref))):
            copy = pltpu.make_async_copy(held.at[:, rows, :], out.at[:, rows, :], sems.at[place, part])
            copy.start()
            copies.append(copy)
    for copy in copies:
        copy.wait()


def call(kernel, name, ins, outs, operands, scratch=(), flops=0, limit=24, places=None):
    size = sum(4 * int(np.prod(o.shape)) for o in outs) + sum(4 * int(np.prod(o.shape)) for o in operands)
    return pl.pallas_call(
        kernel,
        name=name,
        in_specs=ins,
        out_specs=places or [VMEM] * len(outs),
        out_shape=outs,
        scratch_shapes=list(scratch),
        compiler_params=pltpu.CompilerParams(vmem_limit_bytes=limit * 1024 * 1024),
        cost_estimate=pl.CostEstimate(flops=flops, bytes_accessed=size, transcendentals=0),
    )(*operands)


def f32(*shape):
    return jax.ShapeDtypeStruct(shape, jnp.float32)


def bf16(*shape):
    return jax.ShapeDtypeStruct(shape, jnp.bfloat16)


def shards(primal_slab, wave_dual, nuc_dual, l21_weights, nuc_thresh, basis, band_of, margin_width):
    chans = wave_dual.shape[0]
    spec, rows, cols = (lax.axis_size(a) for a in ("spec", "frow", "fcol"))
    senders = rows * cols
    deal = primal_slab.shape[1] // rows
    rank = basis.shape[3]
    bands = l21_weights.shape[0]
    plane = ("fcol", "frow")
    local_basis = basis.reshape(chans, rank).T
    bands_here = band_of.reshape(chans)
    widths = margin_width.reshape(2)

    groups = chans // SLOTS
    block = deal * (chans + groups)
    (packed,) = call(
        functools.partial(pack_kernel, chans=chans, facet_rows=rows, facet_cols=cols, deal=deal),
        "pack", [VMEM], [f32(senders * block, LANES)],
        [primal_slab.reshape(-1, LANES)],
    )
    arrived = lax.all_to_all(
        packed.reshape(senders, block, LANES), plane, split_axis=0, concat_axis=0, tiled=True
    )
    centre, sides = column_operators()
    vertical, across, spread, pick = call(
        prepare_kernel, "prepare", [SMEM] * 3 + [VMEM] * 3,
        [bf16(3 * FACET // 2, 6 * LANES), bf16(SLOTS, 6 * LANES, 2 * LANES),
         f32(rank, chans, 8, LANES), jax.ShapeDtypeStruct((chans, 8, LANES), jnp.int32)],
        [widths, local_basis, bands_here, jnp.asarray(row_operator()), jnp.asarray(centre), jnp.asarray(sides)],
        scratch=[pltpu.VMEM((LANES, 2 * LANES), jnp.float32)],
    )
    strip = f32(chans + groups, EDGE, LANES)
    facet, side, first, second = call(
        functools.partial(unpack_kernel, chans=chans, deal=deal, facet_rows=rows, facet_cols=cols),
        "unpack", [VMEM],
        [f32(chans, FACET, LANES), f32(groups, FACET, LANES), strip, strip],
        [arrived.reshape(-1, LANES)],
    )
    inward = [(i, i - 1 if i % 2 == 0 else i + 1) for i in range(1, rows - 1)]
    first = lax.ppermute(first, "frow", inward)
    second = lax.ppermute(second, "frow", [(i, i ^ 1) for i in range(rows)])
    combined, partial = call(
        functools.partial(project_kernel, chans=chans, rank=rank),
        "project", [VMEM, VMEM, SMEM],
        [f32(chans, FACET, LANES), f32(rank, FACET, LANES)],
        [facet, nuc_dual, local_basis],
        flops=2 * chans * rank * FACET * LANES,
    )
    share = bands * FACET // spec
    chips = spec // 2
    chunks = f32(chips, FACET + share, LANES)
    (columns,) = call(
        functools.partial(columns_kernel, chans=chans),
        "columns", [VMEM] * 3, [bf16(chans, 2, FACET, 2 * LANES)], [facet, side, across],
        flops=2 * chans * 3 * 128 * 256 * 256,
    )
    dual_sum, own, other = call(
        functools.partial(wavelet_kernel, chans=chans),
        "wavelet", [VMEM] * 8,
        [f32(chans, FACET, LANES), chunks, chunks],
        [pick, columns, first, second, vertical, across, partial, wave_dual],
        scratch=[
            pltpu.VMEM((bands * FACET, LANES), jnp.float32),
        ],
        flops=2 * chans * 3 * 192 * 256 * 600,
    )

    def swap(values):
        return lax.ppermute(values, "spec", [(i, i ^ 1) for i in range(spec)])

    def across_chips(values):
        cores = [list(range(core, spec, 2)) for core in range(2)]
        return lax.all_to_all(
            values, "spec", split_axis=0, concat_axis=0, tiled=True, axis_index_groups=cores
        )

    (sums,) = call(pair_kernel, "pair", [VMEM, VMEM], [chunks], [own, swap(other)])
    (weighed,) = call(
        weigh_kernel, "weigh", [VMEM] * 3, [chunks],
        [nuc_thresh.reshape(1, rank), l21_weights.reshape(spec, share, LANES), across_chips(sums)],
    )
    own = across_chips(weighed)
    wave_new, nuc_new = call(
        functools.partial(finish_kernel, chans=chans, rank=rank),
        "finish", [VMEM] * 6,
        [f32(chans, FACET, LANES), f32(chans, FACET, LANES)],
        [spread, pick, combined, dual_sum, own, swap(own)],
        scratch=[
            pltpu.VMEM((spec, FACET + share, LANES), jnp.float32),
            pltpu.VMEM((chans, FACET, LANES), jnp.float32),
            pltpu.VMEM((chans, FACET, LANES), jnp.float32),
            pltpu.SemaphoreType.DMA((2, FACET // share)),
        ],
        flops=2 * chans * rank * FACET * LANES,
        places=[HBM, HBM],
    )
    return (wave_new, nuc_new)


def solution(mesh):
    return jax.shard_map(
        shards,
        mesh=mesh,
        in_specs=(
            P("spec", None, "frow", "fcol", None),
            P("spec", "frow", "fcol"),
            P("spec", "frow", "fcol"),
            P(None, "frow", "fcol"),
            P("frow", "fcol", None),
            P("frow", "fcol", "spec", None),
            P("frow", "fcol", "spec"),
            P("frow", "fcol", None),
        ),
        out_specs=(P("spec", "frow", "fcol"), P("spec", "frow", "fcol")),
        check_vma=False,
    )
```
